256 devices in a mesh: expert: 64 (over x, z, core), mp: 4 (over y).
Axes of the slice: x: 4, y: 4, z: 8, core: 2. Of those that a mesh axis runs over, the one named last changes fastest.
Arguments:
- routes: int32 [8192, 8], P('expert'), may hold values from 0 to 127, all different within a row; in each aligned block of 128 rows (0 to 127, 128 to 255, ...) at most 12 rows name the same one
- routed_hidden: bfloat16 [8192, 8, 1024], P('expert', None, 'mp'), may hold values from -36 to 36
- down_proj: bfloat16 [128, 1024, 3584], P('expert', None, 'mp'), may hold values from -6 to 6
- merge_group: int32 [128], replicated, may hold values from 0 to 63, as said below
Outputs:
- merged: bfloat16 [64, 1024, 3584], P('expert', None, 'mp')
The draws below stay inside these ranges and needn't reach their ends.
Inputs may be any that keep to these rules, and one draw needn't show every extreme that they name: `routes`: among the 128 tokens of one index of the expert axis (aligned blocks of rows) no expert is named more than 12 times, a bound that some block reaches. `merge_group`: every group holds 1 to 3 experts, and some group holds exactly 3.
All inputs are finite; a program needn't handle non-finite values.
Results may differ from the reference program's by a relative error of at most 0.0056.
Values may be sent and summed in bfloat16 or wider, within the bound.
No kernel may reach another device: no remote copies, remote signals or barrier semaphores. Data moves between devices by JAX's collectives and lax.ppermute only.
A program may use at most 128 MiB of HBM per device.

```python
import math
import jax
import jax.numpy as jnp
import numpy as np
from jax import lax

FF = 1024
DW = 3584
TOP = 8
GMAX = 3
TOK_DEV = 128
EXPERTS = 128
GROUPS = 64
TOKENS = 8192
CAP = 12
SLOTS = 768


def draw_routed_hidden(key, part):
    col_key, row_key, base_key = jax.random.split(jax.random.fold_in(key, 17), 3)
    log_lower = math.log(0.3)
    log_upper = math.log(3.0)
    col_scale = jnp.exp(jax.random.uniform(col_key, (FF,), jnp.float32, log_lower, log_upper))
    row_scale = jnp.exp(jax.random.uniform(row_key, (TOKENS, TOP, 1), jnp.float32, log_lower, log_upper))
    base_values = jnp.clip(jax.random.normal(base_key, (TOKENS, TOP, FF), jnp.float32), -4.0, 4.0)
    return (base_values * row_scale * col_scale[None, None, :]).astype(jnp.bfloat16)


def draw_merge_group(key, part):
    kind_key, first_key, shuffle_key = jax.random.split(jax.random.fold_in(key, 29), 3)
    pair_kind = jax.random.randint(kind_key, (GROUPS // 2,), 0, GMAX)
    pair_kind = pair_kind.at[0].set((GMAX - 1) * jax.random.randint(first_key, (), 0, 2))
    group_sizes = jnp.stack([pair_kind + 1, GMAX - pair_kind], axis=1).reshape(GROUPS)
    bounds = jnp.cumsum(group_sizes)
    labels = jnp.sum((bounds[None, :] <= jnp.arange(EXPERTS)[:, None]).astype(jnp.int32), axis=1)
    shuffle = jax.random.permutation(shuffle_key, EXPERTS)
    return labels[shuffle].astype(jnp.int32)


def level_of(rng, shape, cuts, least, top_value):
    gain, own = 1.0, jax.random.fold_in(rng, 6)
    for axis_at, shards_of in cuts:
        draws = jnp.exp(jax.random.uniform(jax.random.fold_in(own, axis_at), (shards_of,), jnp.float32, least / len(cuts), top_value / len(cuts)))
        gain = gain * jnp.repeat(draws, shape[axis_at] // shards_of).reshape([-1 if axis == axis_at else 1 for axis in range(len(shape))])
    return gain


def routed_block(key, own, number, rows, amount, top, bound, slope):
    ranking = jax.random.permutation(key, amount)
    crowded, usual = portions_of(amount, rows * top, bound, slope, True), portions_of(amount, rows * top, bound, slope, False)
    places = jnp.arange(amount)

    def named(tallies, offset_by):
        used = int((tallies > 0).sum())
        fixed = max(1, used // 4)
        passed = fixed + (places - fixed + offset_by * (used - fixed)) % max(1, amount - fixed)
        return jnp.zeros((amount,), jnp.int32).at[ranking[jnp.where(places < fixed, places, passed)]].set(jnp.asarray(tallies, jnp.int32))

    tallies = jnp.where(number % 4 == 0, named(crowded, number // 4), named(usual, number - number // 4 - 1))
    mixed = jax.random.permutation(jax.random.fold_in(own, 3), amount)
    giver, receiver = mixed[0:amount // 2 * 2:2], mixed[1:amount // 2 * 2:2]
    margin = jnp.minimum(tallies[giver] - 1, bound - tallies[receiver]) // 2
    margin = jnp.where((giver == ranking[0]) | (receiver == ranking[0]) | (tallies[receiver] == 0), 0, jnp.maximum(margin, 0))
    passed = jax.random.randint(jax.random.fold_in(own, 4), (amount // 2,), 0, 1 << 20) % (margin + 1)
    tallies = tallies.at[giver].add(-passed).at[receiver].add(passed)
    items = jnp.searchsorted(jnp.cumsum(tallies), jnp.arange(rows * top), side="right").astype(jnp.int32)
    listing = items.reshape(top, rows).T
    listing = listing[jax.random.permutation(jax.random.fold_in(own, 1), rows)]
    offset_by = jax.random.randint(jax.random.fold_in(own, 2), (rows, 1), 0, top)
    return jnp.take_along_axis(listing, (jnp.arange(top)[None, :] + offset_by) % top, axis=1)


def portions_of(count, total, bound, lean, full):
    weights = [(1 << 20) // math.isqrt(standing ** lean) + 1 for standing in range(1, count + 1)]
    largest = bound if full else min(bound, max(-(-total // count), total * weights[0] // sum(weights)))
    least = 1 if total - largest >= count - 1 else 0
    holding, surplus = [largest] + [least] * (count - 1), total - largest - least * (count - 1)
    while surplus > 0:
        candidates = [i for i in range(1, count) if holding[i] < largest] or [i for i in range(1, count) if holding[i] < bound]
        whole, left = sum([weights[i] for i in candidates]), surplus
        for i in candidates:
            addition = min(bound - holding[i], max(1, left * weights[i] // whole), surplus)
            holding[i] = holding[i] + addition
            surplus = surplus - addition
    return np.array(holding)


def centred(rng, extent, width, limit, shards=(), kind=jnp.bfloat16):
    values = jax.random.normal(rng, extent, jnp.float32) * width
    if len(shards) > 0:
        values = level_of(rng, extent, shards, -0.22, 0.18) * values
    return jnp.clip(values, min=-limit, max=limit).astype(kind)


def setup_inputs(seed: int = 0) -> dict:
    key_of = jax.random.split(jax.random.key(seed), 5)
    routes_keys = jax.random.split(jax.random.fold_in(key_of[0], 1), TOKENS // TOK_DEV)
    routes_turns = jax.random.permutation(jax.random.fold_in(key_of[0], 3), TOKENS // TOK_DEV)
    routes = jax.vmap(lambda own, number: routed_block(jax.random.fold_in(key_of[0], 2), own, number, TOK_DEV, EXPERTS, TOP, CAP, 2))(routes_keys, routes_turns).reshape((TOKENS, TOP))
    routed_hidden = draw_routed_hidden(jax.random.fold_in(key_of[4], 71), 0)
    down_proj = centred(key_of[2], (EXPERTS, FF, DW), 1.0, 6.0, ((0, 64), (2, 4)))
    merge_group = draw_merge_group(jax.random.fold_in(key_of[4], 71), 0)
    return {"routes": routes, "routed_hidden": routed_hidden, "down_proj": down_proj, "merge_group": merge_group}


damping = 0.1
epsilon = 1e-05

def slot_rank(labels, label_count):
    onehot = (labels[:, None] == jnp.arange(label_count, dtype=jnp.int32)[None, :]).astype(jnp.int32)
    return jnp.sum(onehot * (jnp.cumsum(onehot, axis=0) - 1), axis=1).astype(jnp.int32)

def member_table(merge_group, group_count):
    expert_total = merge_group.shape[0]
    position = slot_rank(merge_group, group_count)
    slot_table = jnp.full((group_count * GMAX,), -1, jnp.int32)
    slot_table = slot_table.at[merge_group * GMAX + position].set(jnp.arange(expert_total, dtype=jnp.int32))
    return slot_table.reshape(group_count, GMAX)

def solve_group(gram_sum, partial_value):
    order_size = gram_sum.shape[0]
    ridge_term = damping * jnp.trace(gram_sum) / order_size + epsilon
    system = gram_sum + ridge_term * jnp.eye(order_size, dtype=jnp.float32)
    factor = jnp.linalg.cholesky(system)
    return jax.scipy.linalg.cho_solve((factor, True), partial_value)

def reference(routes, routed_hidden, down_proj, merge_group):
    row_count = TOKENS * TOP
    targets = routes.reshape(row_count).astype(jnp.int32)
    padded = jnp.concatenate([routed_hidden.reshape(row_count, FF), jnp.zeros((1, FF), routed_hidden.dtype)], axis=0)
    sorted_rows = jnp.argsort(targets, stable=True).astype(jnp.int32)
    counts = jnp.zeros((EXPERTS,), jnp.int32).at[targets].add(1)
    starts = jnp.cumsum(counts).astype(jnp.int32) - counts
    places = jnp.arange(SLOTS, dtype=jnp.int32)
    members = member_table(merge_group.astype(jnp.int32), GROUPS)
    highest = lax.Precision.HIGHEST

    def expert_terms(expert):
        position = starts[expert] + places
        valid_slot = places < counts[expert]
        source_row = jnp.where(valid_slot, sorted_rows[jnp.minimum(position, row_count - 1)], row_count)
        expert_rows = padded[source_row].astype(jnp.float32)
        weight = down_proj[expert].astype(jnp.float32)
        gram_term = jnp.dot(expert_rows.T, expert_rows, precision=highest)
        projected = jnp.dot(expert_rows, weight, precision=highest)
        projected = lax.optimization_barrier(projected.astype(jnp.bfloat16)).astype(jnp.float32)
        product = jnp.dot(expert_rows.T, projected, precision=highest)
        return (gram_term, product)

    def empty_terms(expert):
        return (jnp.zeros((FF, FF), jnp.float32), jnp.zeros((FF, DW), jnp.float32))

    def merge_one(group_index):
        gram_sum = jnp.zeros((FF, FF), jnp.float32)
        partial_value = jnp.zeros((FF, DW), jnp.float32)
        for member_slot in range(GMAX):
            expert = members[group_index, member_slot]
            gram_term, product = lax.cond(expert >= 0, expert_terms, empty_terms, jnp.maximum(expert, 0))
            gram_sum = gram_sum + gram_term
            partial_value = partial_value + product
        return solve_group(gram_sum, partial_value).astype(jnp.bfloat16)
    return lax.map(merge_one, jnp.arange(GROUPS, dtype=jnp.int32))
```

```python
import jax
import jax.numpy as jnp
from jax import lax
from jax.experimental import pallas as pl
from jax.experimental.pallas import tpu as pltpu
from jax.sharding import PartitionSpec as P

GMAX = 3
BLK = 256
damping = 0.1
epsilon = 1e-05
F32 = jnp.float32
BF16 = jnp.bfloat16


def sweep_counts():
    gaps, delta = [], 1e-3
    for _ in range(16):
        gaps.append(1.0 - delta)
        if 2.0 * delta / (1.0 + delta) > 2.0 - 2.0 / GAIN_MAX:
            delta = (1.0 - (1.0 - delta) / GAIN_MAX) ** 0.5
        else:
            delta = (2.0 * delta / (1.0 + delta)) ** 0.5
    return gaps


GAIN_MAX = 1.85
NEWTON_GAPS = sweep_counts()


def halves(value):
    high = value.astype(BF16)
    return high, (value - high.astype(F32)).astype(BF16)


def dot(a, b):
    return jnp.dot(a, b, preferred_element_type=F32)


def dot3(a, b):
    (ah, al), (bh, bl) = a, b
    return dot(ah, bh) + (dot(ah, bl) + dot(al, bh))


def thirds(value):
    high = value.astype(BF16)
    rest = value - high.astype(F32)
    mid = rest.astype(BF16)
    return high, mid, (rest - mid.astype(F32)).astype(BF16)


def dot6(a, b):
    (ah, am, al), (bh, bm, bl) = a, b
    small = dot(am, bm) + (dot(ah, bl) + dot(al, bh))
    return dot(ah, bh) + (dot(ah, bm) + dot(am, bh) + small)


def block_inverse(block, lower):
    size = block.shape[0]
    upper = jnp.max(jnp.sum(jnp.abs(block), axis=1, keepdims=True))
    gap = 2.0 * lower / (lower + upper)
    steps = jnp.int32(0)
    for edge in NEWTON_GAPS:
        steps = steps + (gap < edge).astype(jnp.int32)
    rows = lax.broadcasted_iota(jnp.int32, (size, size), 0)
    cols = lax.broadcasted_iota(jnp.int32, (size, size), 1)
    total = jnp.full((1, size), lower + upper, F32)
    start = jnp.where(rows == cols, 2.0 / total, 0.0)
    block_parts = thirds(block)

    def step(_, carry):
        guess, delta = carry
        parts = halves(guess)
        image = dot3(block_parts[:2], parts)
        gain = jnp.minimum(2.0 / (2.0 - delta * delta), GAIN_MAX)
        guess = gain * (2.0 * guess - dot3(parts, halves(image)))
        return guess, 1.0 - gain * (1.0 - delta * delta)

    guess, _ = lax.fori_loop(0, steps, step, (start, 1.0 - 2.0 * lower / total))
    parts = thirds(guess)
    return 2.0 * guess - dot6(parts, thirds(dot6(block_parts, parts)))


def solve_kernel(rows_ref, out_ref, gram_ref, sys_ref, high_ref, low_ref):
    layers, slots, width = rows_ref.shape
    count = width // BLK

    def span(index):
        return pl.ds(pl.multiple_of(index * BLK, BLK), BLK)

    def gram_block(index, carry):
        layer, i, j = index // (count * count), index // count % count, index % count
        gram_ref[layer, span(i), span(j)] = lax.dot_general(
            rows_ref[layer, :, span(i)],
            rows_ref[layer, :, span(j)],
            (((0,), (0,)), ((), ())),
            preferred_element_type=F32,
        )
        return carry

    lax.fori_loop(0, layers * count * count, gram_block, 0)
    diag = lax.broadcasted_iota(jnp.int32, (BLK, BLK), 0) == lax.broadcasted_iota(
        jnp.int32, (BLK, BLK), 1
    )
    trace = jnp.float32(0)
    for i in range(count):
        here = slice(i * BLK, (i + 1) * BLK)
        block = gram_ref[0, here, here] + gram_ref[1, here, here] + gram_ref[2, here, here]
        trace = trace + jnp.sum(jnp.where(diag, block, 0.0))
    ridge = damping * trace / width + epsilon

    def system_block(i, carry):
        value = gram_ref[0, span(i), :] + gram_ref[1, span(i), :] + gram_ref[2, span(i), :]
        shape = (BLK, width)
        on = lax.broadcasted_iota(jnp.int32, shape, 0) + i * BLK == lax.broadcasted_iota(
            jnp.int32, shape, 1
        )
        sys_ref[span(i), :] = value + jnp.where(on, ridge, 0.0)
        return carry

    lax.fori_loop(0, count, system_block, 0)

    def sweep(k, carry):
        inverse = block_inverse(sys_ref[span(k), span(k)], ridge)
        inverse_parts = thirds(inverse)
        panel = dot6(inverse_parts, thirds(sys_ref[span(k), :]))
        panel_parts = thirds(panel)

        def eliminate(i, inner):
            @pl.when(i != k)
            def _():
                left = thirds(sys_ref[span(i), span(k)])
                sys_ref[span(i), :] = sys_ref[span(i), :] - dot6(left, panel_parts)
                sys_ref[span(i), span(k)] = dot6(left, inverse_parts)

            return inner

        lax.fori_loop(0, count, eliminate, 0)
        sys_ref[span(k), :] = panel
        sys_ref[span(k), span(k)] = -inverse
        return carry

    lax.fori_loop(0, count, sweep, 0)

    def split_gram(i, carry):
        for layer in range(1, layers):
            high, low = halves(gram_ref[layer, span(i), :])
            high_ref[layer - 1, span(i), :] = high
            low_ref[layer - 1, span(i), :] = low
        return carry

    lax.fori_loop(0, count, split_gram, 0)

    def member_block(index, carry):
        i, j = index // count, index % count
        inverse = halves(-sys_ref[span(i), :])
        first = dot3(inverse, (high_ref[0, :, span(j)], low_ref[0, :, span(j)]))
        second = dot3(inverse, (high_ref[1, :, span(j)], low_ref[1, :, span(j)]))
        rest = ridge * sys_ref[span(i), span(j)] - first - second
        rest = rest + jnp.where(diag & (i == j), 1.0, 0.0)
        out_ref[0, span(i), span(j)] = rest.astype(BF16)
        out_ref[1, span(i), span(j)] = first.astype(BF16)
        out_ref[2, span(i), span(j)] = second.astype(BF16)
        return carry

    lax.fori_loop(0, count * count, member_block, 0)


def member_maps(rows):
    layers, slots, width = rows.shape
    return pl.pallas_call(
        solve_kernel,
        out_shape=jax.ShapeDtypeStruct((layers, width, width), BF16),
        in_specs=[pl.BlockSpec(memory_space=pltpu.VMEM)],
        out_specs=pl.BlockSpec(memory_space=pltpu.VMEM),
        scratch_shapes=[
            pltpu.VMEM((layers, width, width), F32),
            pltpu.VMEM((width, width), F32),
            pltpu.VMEM((layers - 1, width, width), BF16),
            pltpu.VMEM((layers - 1, width, width), BF16),
        ],
        compiler_params=pltpu.CompilerParams(vmem_limit_bytes=56 * 1024 * 1024),
        cost_estimate=pl.CostEstimate(
            flops=40_000_000_000, bytes_accessed=12_000_000, transcendentals=0
        ),
        name="member_maps",
    )(rows)


CHUNK = 40


def pack_kernel(cap, routes_ref, column_ref, line_ref, rows_ref, out_ref):
    experts = column_ref.shape[0]
    count = routes_ref.shape[1]
    square = (experts, experts)
    earlier = lax.broadcasted_iota(jnp.int32, square, 1) < lax.broadcasted_iota(
        jnp.int32, square, 0
    )
    same = (column_ref[...] == line_ref[...]) & earlier
    rank = jnp.sum(jnp.where(same, 1.0, 0.0), axis=1, keepdims=True)
    base = column_ref[...].astype(F32) * CHUNK + rank * cap
    hit = lax.broadcasted_iota(jnp.int32, (experts, count), 0) == routes_ref[...]
    onehot = jnp.where(hit, 1.0, 0.0).astype(BF16)
    order = lax.broadcasted_iota(jnp.int32, (count, count), 0) < lax.broadcasted_iota(
        jnp.int32, (count, count), 1
    )
    before = dot(onehot, jnp.where(order, 1.0, 0.0).astype(BF16))
    slot = jnp.sum(jnp.where(hit, base + before, 0.0), axis=0, keepdims=True)
    slot = slot.astype(jnp.int32)

    def place(index, carry):
        here = pl.multiple_of(index * BLK, BLK)
        wanted = lax.broadcasted_iota(jnp.int32, (BLK, count), 0) + here
        pick = jnp.where(wanted == slot, 1.0, 0.0).astype(BF16)
        out_ref[pl.ds(here, BLK), :] = dot(pick, rows_ref[...]).astype(BF16)
        return carry

    lax.fori_loop(0, out_ref.shape[0] // BLK, place, 0)


def pack_rows(routes, merge_group, rows, cap, group_count):
    count, width = rows.shape
    experts = merge_group.shape[0]
    return pl.pallas_call(
        lambda *refs: pack_kernel(cap, *refs),
        out_shape=jax.ShapeDtypeStruct((group_count * CHUNK, width), BF16),
        in_specs=[pl.BlockSpec(memory_space=pltpu.VMEM)] * 4,
        out_specs=pl.BlockSpec(memory_space=pltpu.VMEM),
        compiler_params=pltpu.CompilerParams(vmem_limit_bytes=32 * 1024 * 1024),
        cost_estimate=pl.CostEstimate(
            flops=2_000_000_000, bytes_accessed=2_000_000, transcendentals=0
        ),
        name="pack_rows",
    )(routes.reshape(1, count), merge_group[:, None], merge_group[None, :], rows)


def pick_kernel(members_ref, pieces_ref, out_ref):
    groups, layers = out_ref.shape[:2]
    first = pl.program_id(0) * groups

    def copy_group(index, carry):
        for layer in range(layers):
            member = members_ref[(first + index) * layers + layer]
            out_ref[index, layer] = pieces_ref[member]
        return carry

    lax.fori_loop(0, groups, copy_group, 0)


def pick_members(pieces, members, group_count):
    experts, depth, width = pieces.shape
    part = group_count // 4
    return pl.pallas_call(
        pick_kernel,
        out_shape=jax.ShapeDtypeStruct((group_count, GMAX, depth, width), BF16),
        grid_spec=pltpu.PrefetchScalarGridSpec(
            num_scalar_prefetch=1,
            grid=(4,),
            in_specs=[pl.BlockSpec((experts, depth, width), lambda i, m: (0, 0, 0))],
            out_specs=pl.BlockSpec((part, GMAX, depth, width), lambda i, m: (i, 0, 0, 0)),
        ),
        compiler_params=pltpu.CompilerParams(vmem_limit_bytes=32 * 1024 * 1024),
        cost_estimate=pl.CostEstimate(
            flops=0, bytes_accessed=9_200_000, transcendentals=0
        ),
        name="pick_members",
    )(members, pieces)


def merge_kernel(maps_ref, weights_ref, out_ref, total_ref):
    layer = pl.program_id(0)
    groups, depth, width = weights_ref.shape
    size = out_ref.shape[0]

    def strip(index, carry):
        here = pl.ds(pl.multiple_of(index * BLK, BLK), BLK)
        weights = weights_ref[...].reshape(groups * depth, width)
        value = dot(maps_ref[here, :], weights)

        @pl.when(layer == 0)
        def _():
            total_ref[here, :] = value

        @pl.when(layer == 1)
        def _():
            total_ref[here, :] = total_ref[here, :] + value

        @pl.when(layer == 2)
        def _():
            out_ref[here, :] = (total_ref[here, :] + value).astype(BF16)

        return carry

    lax.fori_loop(0, size // BLK, strip, 0)


def merge_weights(maps, weights):
    layers, size, _ = maps.shape
    groups, _, depth, width = weights.shape
    return pl.pallas_call(
        merge_kernel,
        out_shape=jax.ShapeDtypeStruct((size, width), BF16),
        grid=(layers,),
        in_specs=[
            pl.BlockSpec((None, size, size), lambda l: (l, 0, 0)),
            pl.BlockSpec((groups, None, depth, width), lambda l: (0, l, 0, 0)),
        ],
        out_specs=pl.BlockSpec((size, width), lambda l: (0, 0)),
        scratch_shapes=[pltpu.VMEM((size, width), F32)],
        compiler_params=pltpu.CompilerParams(vmem_limit_bytes=40 * 1024 * 1024),
        cost_estimate=pl.CostEstimate(
            flops=5_600_000_000, bytes_accessed=13_000_000, transcendentals=0
        ),
        name="merge_weights",
    )(maps, weights)


def member_table(merge_group, group_count):
    experts = merge_group.shape[0]
    index = jnp.arange(experts, dtype=jnp.int32)
    earlier = index[None, :] < index[:, None]
    rank = jnp.sum((merge_group[:, None] == merge_group[None, :]) & earlier, axis=1)
    place = merge_group * GMAX + rank
    wanted = jnp.arange(group_count * GMAX, dtype=jnp.int32)
    return jnp.sum(jnp.where(place[None, :] == wanted[:, None], index[None, :], 0), axis=1)


def on_device(routes, routed_hidden, down_proj, merge_group):
    group_count = lax.axis_size("expert")
    local_count, full_width, out_part = down_proj.shape
    tok_count, top_count, hidden_part = routed_hidden.shape
    row_count = tok_count * top_count
    experts = merge_group.shape[0]
    cap = 3 * row_count // (2 * experts)
    depth = full_width // group_count

    pieces = down_proj.reshape(local_count, group_count, depth, out_part)
    pieces = lax.all_to_all(
        pieces.transpose(1, 0, 2, 3), "expert", split_axis=0, concat_axis=0, tiled=True
    )
    rows = routed_hidden.reshape(row_count, hidden_part)
    packed = pack_rows(routes, merge_group, rows, cap, group_count)
    packed = packed.reshape(group_count, CHUNK, hidden_part)
    arrived = lax.all_to_all(packed, "expert", split_axis=0, concat_axis=0, tiled=True)
    arrived = arrived[:, : GMAX * cap].reshape(group_count, GMAX, cap, hidden_part)
    arrived = arrived.transpose(1, 0, 2, 3).reshape(GMAX, group_count * cap, hidden_part)
    member_rows = lax.all_gather(arrived, "mp", axis=2, tiled=True)

    members = member_table(merge_group, group_count)
    picked = pick_members(
        pieces.reshape(experts, depth, out_part), members, group_count
    )
    weights = lax.all_to_all(picked, "expert", split_axis=0, concat_axis=0, tiled=True)
    maps = member_maps(member_rows)
    merged = merge_weights(maps, weights)
    return merged.reshape(1, full_width, out_part)


def solution(mesh):
    return jax.shard_map(
        on_device,
        mesh=mesh,
        in_specs=(P("expert", None), P("expert", None, "mp"), P("expert", None, "mp"), P()),
        out_specs=P("expert", None, "mp"),
        check_vma=False,
    )
```

```python
import jax
import jax.numpy as jnp
from jax import lax
from jax.experimental import pallas as pl
from jax.experimental.pallas import tpu as pltpu
from jax.sharding import PartitionSpec as P

GMAX = 3
BLK = 256
damping = 0.1
epsilon = 1e-05
F32 = jnp.float32
BF16 = jnp.bfloat16


def sweep_counts():
    gaps, delta = [], 1e-3
    for _ in range(16):
        gaps.append(1.0 - delta)
        if 2.0 * delta / (1.0 + delta) > 2.0 - 2.0 / GAIN_MAX:
            delta = (1.0 - (1.0 - delta) / GAIN_MAX) ** 0.5
        else:
            delta = (2.0 * delta / (1.0 + delta)) ** 0.5
    return gaps


GAIN_MAX = 1.85
NEWTON_GAPS = sweep_counts()


def halves(value):
    high = value.astype(BF16)
    return high, (value - high.astype(F32)).astype(BF16)


def dot(a, b):
    return jnp.dot(a, b, preferred_element_type=F32)


def dot3(a, b):
    (ah, al), (bh, bl) = a, b
    return dot(ah, bh) + (dot(ah, bl) + dot(al, bh))


def thirds(value):
    high = value.astype(BF16)
    rest = value - high.astype(F32)
    mid = rest.astype(BF16)
    return high, mid, (rest - mid.astype(F32)).astype(BF16)


def dot6(a, b):
    (ah, am, al), (bh, bm, bl) = a, b
    small = dot(am, bm) + (dot(ah, bl) + dot(al, bh))
    return dot(ah, bh) + (dot(ah, bm) + dot(am, bh) + small)


def block_inverse(block, lower):
    size = block.shape[0]
    upper = jnp.max(jnp.sum(jnp.abs(block), axis=1, keepdims=True))
    gap = 2.0 * lower / (lower + upper)
    steps = jnp.int32(0)
    for edge in NEWTON_GAPS:
        steps = steps + (gap < edge).astype(jnp.int32)
    rows = lax.broadcasted_iota(jnp.int32, (size, size), 0)
    cols = lax.broadcasted_iota(jnp.int32, (size, size), 1)
    total = jnp.full((1, size), lower + upper, F32)
    start = jnp.where(rows == cols, 2.0 / total, 0.0)
    block_parts = thirds(block)

    def step(_, carry):
        guess, delta = carry
        parts = halves(guess)
        image = dot3(block_parts[:2], parts)
        gain = jnp.minimum(2.0 / (2.0 - delta * delta), GAIN_MAX)
        guess = gain * (2.0 * guess - dot3(parts, halves(image)))
        return guess, 1.0 - gain * (1.0 - delta * delta)

    guess, _ = lax.fori_loop(0, steps, step, (start, 1.0 - 2.0 * lower / total))
    parts = thirds(guess)
    return 2.0 * guess - dot6(parts, thirds(dot6(block_parts, parts)))


TILE = 8
HELD = 3
OWNED = 5


def slot_kernel(routes_ref, bases_ref, rows_ref, out_ref, slot_ref):
    experts = bases_ref.shape[0]
    count = routes_ref.shape[1]
    hit = lax.broadcasted_iota(jnp.int32, (experts, count), 0) == routes_ref[...]
    onehot = jnp.where(hit, 1.0, 0.0).astype(BF16)
    order = lax.broadcasted_iota(jnp.int32, (count, count), 0) < lax.broadcasted_iota(
        jnp.int32, (count, count), 1
    )
    before = dot(onehot, jnp.where(order, 1.0, 0.0).astype(BF16))
    bases = bases_ref[...].astype(F32)
    place = before + jnp.where(before < TILE, bases[:, 0:1], bases[:, 1:2])
    slot = jnp.sum(jnp.where(hit, place, 0.0), axis=0, keepdims=True)
    slot_ref[...] = slot.astype(jnp.int32)

    def fill(index, carry):
        here = pl.multiple_of(index * BLK, BLK)
        wanted = lax.broadcasted_iota(jnp.int32, (BLK, count), 0) + here
        pick = jnp.where(wanted == slot_ref[...], 1.0, 0.0).astype(BF16)
        out_ref[pl.ds(here, BLK), :] = dot(pick, rows_ref[...]).astype(BF16)
        return carry

    lax.fori_loop(0, out_ref.shape[0] // BLK, fill, 0)


def pack_rows(routes, bases, rows, slots, name):
    count, width = rows.shape
    return pl.pallas_call(
        slot_kernel,
        out_shape=jax.ShapeDtypeStruct((slots, width), BF16),
        in_specs=[pl.BlockSpec(memory_space=pltpu.VMEM)] * 3,
        out_specs=pl.BlockSpec(memory_space=pltpu.VMEM),
        scratch_shapes=[pltpu.VMEM((1, count), jnp.int32)],
        compiler_params=pltpu.CompilerParams(vmem_limit_bytes=32 * 1024 * 1024),
        cost_estimate=pl.CostEstimate(
            flops=3_000_000_000, bytes_accessed=2_000_000, transcendentals=0
        ),
        name=name,
    )(routes, bases, rows)


def project_kernel(rows_ref, weights_ref, out_ref):
    parts, blocks = rows_ref.shape[:2]
    width = out_ref.shape[3]
    step = BLK // TILE
    upper = lax.broadcasted_iota(jnp.int32, (BLK, 1), 0) % TILE < TILE // 2

    def strip(index, carry):
        here = pl.ds(index * step, step)
        for tile in range(HELD):
            rows = jnp.concatenate(
                [rows_ref[m, here, tile].reshape(BLK, -1) for m in range(parts)], axis=1
            )
            if tile < 2:
                value = dot(rows, weights_ref[tile])
            else:
                none = jnp.zeros_like(rows)
                value = dot(jnp.where(upper, rows, none), weights_ref[0])
                value = value + dot(jnp.where(upper, none, rows), weights_ref[1])
            out_ref[here, tile] = value.astype(BF16).reshape(step, TILE, width)
        return carry

    lax.fori_loop(0, blocks // step, strip, 0)


def project_rows(rows, weights):
    blocks = rows.shape[1]
    width = weights.shape[2]
    return pl.pallas_call(
        project_kernel,
        out_shape=jax.ShapeDtypeStruct((blocks, HELD, TILE, width), BF16),
        in_specs=[pl.BlockSpec(memory_space=pltpu.VMEM)] * 2,
        out_specs=pl.BlockSpec(memory_space=pltpu.VMEM),
        compiler_params=pltpu.CompilerParams(vmem_limit_bytes=40 * 1024 * 1024),
        cost_estimate=pl.CostEstimate(
            flops=4_000_000_000, bytes_accessed=10_000_000, transcendentals=0
        ),
        name="project_rows",
    )(rows, weights)


def regroup_kernel(members_ref, held_ref, out_ref):
    groups = out_ref.shape[0]
    first = pl.program_id(0) * groups
    width = out_ref.shape[3]
    upper = lax.broadcasted_iota(jnp.int32, (TILE, width), 0) < TILE // 2

    def regroup(index, carry):
        ends = []
        for layer in range(GMAX):
            member = members_ref[(first + index) * GMAX + layer]
            holder, local = member // 2, member % 2
            out_ref[index, layer] = held_ref[holder, local]
            end = held_ref[holder, 2].astype(F32)
            turned = pltpu.roll(end, TILE // 2, 0)
            ends.append(jnp.where(local == layer % 2, end, turned))
        out_ref[index, 3] = jnp.where(upper, ends[0], ends[1]).astype(BF16)
        out_ref[index, 4] = jnp.where(upper, ends[2], 0.0).astype(BF16)
        return carry

    lax.fori_loop(0, groups, regroup, 0)


def regroup_rows(held, members):
    group_count, _, _, width = held.shape
    part = group_count // 4
    return pl.pallas_call(
        regroup_kernel,
        out_shape=jax.ShapeDtypeStruct((group_count, OWNED, TILE, width), BF16),
        grid_spec=pltpu.PrefetchScalarGridSpec(
            num_scalar_prefetch=1,
            grid=(4,),
            in_specs=[pl.BlockSpec(held.shape, lambda i, m: (0, 0, 0, 0))],
            out_specs=pl.BlockSpec((part, OWNED, TILE, width), lambda i, m: (i, 0, 0, 0)),
        ),
        compiler_params=pltpu.CompilerParams(vmem_limit_bytes=32 * 1024 * 1024),
        cost_estimate=pl.CostEstimate(
            flops=0, bytes_accessed=7_500_000, transcendentals=0
        ),
        name="regroup_rows",
    )(members, held)


def invert_kernel(rows_ref, after_ref, high_ref, low_ref, turned_ref, sys_ref):
    del after_ref
    count, slots, _ = rows_ref.shape
    width = count * BLK
    diag = lax.broadcasted_iota(jnp.int32, (BLK, BLK), 0) == lax.broadcasted_iota(
        jnp.int32, (BLK, BLK), 1
    )

    def span(index):
        return pl.ds(pl.multiple_of(index * BLK, BLK), BLK)

    def turn(i, carry):
        turned_ref[span(i), :] = rows_ref[i].T
        return carry

    lax.fori_loop(0, count, turn, 0)

    def gram_block(index, carry):
        i, j = index // count, index % count
        sys_ref[span(i), span(j)] = dot(turned_ref[span(i), :], rows_ref[j])
        return carry

    lax.fori_loop(0, count * count, gram_block, 0)
    trace = jnp.float32(0)
    for i in range(count):
        here = slice(i * BLK, (i + 1) * BLK)
        trace = trace + jnp.sum(jnp.where(diag, sys_ref[here, here], 0.0))
    ridge = damping * trace / width + epsilon
    for i in range(count):
        here = slice(i * BLK, (i + 1) * BLK)
        sys_ref[here, here] = sys_ref[here, here] + jnp.where(diag, ridge, 0.0)

    def sweep(k, carry):
        inverse = block_inverse(sys_ref[span(k), span(k)], ridge)
        inverse_parts = thirds(inverse)
        panel = dot6(inverse_parts, thirds(sys_ref[span(k), :]))
        panel_parts = thirds(panel)

        def eliminate(i, inner):
            @pl.when(i != k)
            def _():
                left = thirds(sys_ref[span(i), span(k)])
                sys_ref[span(i), :] = sys_ref[span(i), :] - dot6(left, panel_parts)
                sys_ref[span(i), span(k)] = dot6(left, inverse_parts)

            return inner

        lax.fori_loop(0, count, eliminate, 0)
        sys_ref[span(k), :] = panel
        sys_ref[span(k), span(k)] = -inverse
        return carry

    lax.fori_loop(0, count, sweep, 0)

    def split(i, carry):
        high, low = halves(-sys_ref[span(i), :])
        high_ref[span(i), :] = high
        low_ref[span(i), :] = low
        return carry

    lax.fori_loop(0, count, split, 0)


def invert_gram(rows, after):
    count, slots, _ = rows.shape
    width = count * BLK
    square = jax.ShapeDtypeStruct((width, width), BF16)
    return pl.pallas_call(
        invert_kernel,
        out_shape=(square, square, jax.ShapeDtypeStruct((width, slots), BF16)),
        in_specs=[
            pl.BlockSpec(memory_space=pltpu.VMEM),
            pl.BlockSpec(memory_space=pl.ANY),
        ],
        out_specs=[pl.BlockSpec(memory_space=pltpu.VMEM)] * 3,
        scratch_shapes=[pltpu.VMEM((width, width), F32)],
        compiler_params=pltpu.CompilerParams(vmem_limit_bytes=40 * 1024 * 1024),
        cost_estimate=pl.CostEstimate(
            flops=60_000_000_000, bytes_accessed=16_000_000, transcendentals=0
        ),
        name="invert_gram",
    )(rows, after)


def merge_kernel(turned_ref, projected_ref, high_ref, low_ref, out_ref, first_ref, second_ref):
    size = out_ref.shape[0]

    def span(index):
        return pl.ds(pl.multiple_of(index * BLK, BLK), BLK)

    def gather(i, carry):
        high, low = halves(dot(turned_ref[span(i), :], projected_ref[...]))
        first_ref[span(i), :] = high
        second_ref[span(i), :] = low
        return carry

    lax.fori_loop(0, size // BLK, gather, 0)

    def strip(i, carry):
        inverse = (high_ref[span(i), :], low_ref[span(i), :])
        value = dot3(inverse, (first_ref[...], second_ref[...]))
        out_ref[span(i), :] = value.astype(BF16)
        return carry

    lax.fori_loop(0, size // BLK, strip, 0)


def merge_rows(turned, projected, high, low):
    size = turned.shape[0]
    width = projected.shape[1]
    return pl.pallas_call(
        merge_kernel,
        out_shape=jax.ShapeDtypeStruct((size, width), BF16),
        in_specs=[pl.BlockSpec(memory_space=pltpu.VMEM)] * 4,
        out_specs=pl.BlockSpec(memory_space=pltpu.VMEM),
        scratch_shapes=[pltpu.VMEM((size, width), BF16)] * 2,
        compiler_params=pltpu.CompilerParams(vmem_limit_bytes=40 * 1024 * 1024),
        cost_estimate=pl.CostEstimate(
            flops=10_300_000_000, bytes_accessed=16_000_000, transcendentals=0
        ),
        name="merge_rows",
    )(turned, projected, high, low)


def member_places(merge_group, group_count):
    experts = merge_group.shape[0]
    index = jnp.arange(experts, dtype=jnp.int32)
    earlier = index[None, :] < index[:, None]
    rank = jnp.sum(
        (merge_group[:, None] == merge_group[None, :]) & earlier, axis=1, dtype=jnp.int32
    )
    place = merge_group * GMAX + rank
    wanted = jnp.arange(group_count * GMAX, dtype=jnp.int32)
    members = jnp.sum(jnp.where(place[None, :] == wanted[:, None], index[None, :], 0), axis=1)
    chunk = merge_group * (OWNED * TILE)
    bases = [chunk + rank * TILE, chunk + GMAX * TILE + rank * (TILE // 2) - TILE]
    return members, jnp.stack(bases, axis=1)


def exchange(rows):
    return lax.all_to_all(rows, "expert", split_axis=0, concat_axis=0, tiled=True)


def on_device(routes, routed_hidden, down_proj, merge_group):
    group_count = lax.axis_size("expert")
    parts = lax.axis_size("mp")
    full_width, out_part = down_proj.shape[1:]
    tok_count, top_count, hidden_part = routed_hidden.shape
    row_count = tok_count * top_count
    experts = merge_group.shape[0]

    rows = routed_hidden.reshape(row_count, hidden_part)
    targets = routes.reshape(1, row_count)
    index = jnp.arange(experts, dtype=jnp.int32)
    chunk, local = index // 2 * (HELD * TILE), index % 2
    held_bases = jnp.stack(
        [chunk + local * TILE, chunk + 2 * TILE + local * (TILE // 2) - TILE], axis=1
    )
    members, owned_bases = member_places(merge_group, group_count)

    to_holder = pack_rows(
        targets, held_bases, rows, group_count * HELD * TILE, "pack_held"
    ).reshape(group_count, HELD * TILE, hidden_part)
    to_owner = pack_rows(
        targets, owned_bases, rows, group_count * OWNED * TILE, "pack_owned"
    ).reshape(group_count, OWNED * TILE, hidden_part)
    at_holder = exchange(to_holder)
    at_holder, to_owner = lax.optimization_barrier((at_holder, to_owner))
    held = lax.all_gather(at_holder, "mp", axis=0)
    at_owner = exchange(to_owner)

    projected = project_rows(
        held.reshape(parts, group_count, HELD, TILE, hidden_part), down_proj
    )
    at_owner, projected = lax.optimization_barrier((at_owner, projected))
    home = exchange(projected.reshape(group_count, HELD * TILE, out_part))
    owned = lax.all_gather(at_owner, "mp", axis=0)
    regrouped = regroup_rows(home.reshape(group_count, HELD, TILE, out_part), members)
    regrouped = regrouped.reshape(group_count, OWNED * TILE, out_part)
    arrived = exchange(regrouped)

    slots = group_count * OWNED * TILE
    high, low, turned = invert_gram(owned.reshape(parts, slots, hidden_part), regrouped)
    merged = merge_rows(turned, arrived.reshape(slots, out_part), high, low)
    return merged.reshape(1, full_width, out_part)


def solution(mesh):
    return jax.shard_map(
        on_device,
        mesh=mesh,
        in_specs=(P("expert", None), P("expert", None, "mp"), P("expert", None, "mp"), P()),
        out_specs=P("expert", None, "mp"),
        check_vma=False,
    )
```

```python
import jax
import jax.numpy as jnp
from jax import lax
from jax.experimental import pallas as pl
from jax.experimental.pallas import tpu as pltpu
from jax.sharding import PartitionSpec as P

GMAX = 3
BLK = 256
damping = 0.1
epsilon = 1e-05
F32 = jnp.float32
BF16 = jnp.bfloat16


def sweep_counts():
    gaps, delta = [], 1e-3
    for _ in range(16):
        gaps.append(1.0 - delta)
        if 2.0 * delta / (1.0 + delta) > 2.0 - 2.0 / GAIN_MAX:
            delta = (1.0 - (1.0 - delta) / GAIN_MAX) ** 0.5
        else:
            delta = (2.0 * delta / (1.0 + delta)) ** 0.5
    return gaps


GAIN_MAX = 1.85
NEWTON_GAPS = sweep_counts()


def halves(value):
    high = value.astype(BF16)
    return high, (value - high.astype(F32)).astype(BF16)


def dot(a, b):
    return jnp.dot(a, b, preferred_element_type=F32)


def dot3(a, b):
    (ah, al), (bh, bl) = a, b
    return dot(ah, bh) + (dot(ah, bl) + dot(al, bh))


def thirds(value):
    high = value.astype(BF16)
    rest = value - high.astype(F32)
    mid = rest.astype(BF16)
    return high, mid, (rest - mid.astype(F32)).astype(BF16)


def dot6(a, b):
    (ah, am, al), (bh, bm, bl) = a, b
    small = dot(am, bm) + (dot(ah, bl) + dot(al, bh))
    return dot(ah, bh) + (dot(ah, bm) + dot(am, bh) + small)


def block_inverse(block, lower):
    size = block.shape[0]
    upper = jnp.max(jnp.sum(jnp.abs(block), axis=1, keepdims=True))
    gap = 2.0 * lower / (lower + upper)
    steps = jnp.int32(0)
    for edge in NEWTON_GAPS:
        steps = steps + (gap < edge).astype(jnp.int32)
    rows = lax.broadcasted_iota(jnp.int32, (size, size), 0)
    cols = lax.broadcasted_iota(jnp.int32, (size, size), 1)
    total = jnp.full((1, size), lower + upper, F32)
    start = jnp.where(rows == cols, 2.0 / total, 0.0)
    block_parts = thirds(block)

    def step(_, carry):
        guess, delta = carry
        parts = halves(guess)
        image = dot3(block_parts[:2], parts)
        gain = jnp.minimum(2.0 / (2.0 - delta * delta), GAIN_MAX)
        guess = gain * (2.0 * guess - dot3(parts, halves(image)))
        return guess, 1.0 - gain * (1.0 - delta * delta)

    guess, _ = lax.fori_loop(0, steps, step, (start, 1.0 - 2.0 * lower / total))
    parts = thirds(guess)
    return 2.0 * guess - dot6(parts, thirds(dot6(block_parts, parts)))


TILE = 8
HELD = 3
OWNED = 5
KEPT = 4
LANES = 128
VMEM_GRANT = 58 * 1024 * 1024


def slot_kernel(routes_ref, bases_ref, rows_ref, out_ref, slot_ref):
    experts = bases_ref.shape[0]
    count = routes_ref.shape[1]
    hit = lax.broadcasted_iota(jnp.int32, (experts, count), 0) == routes_ref[...]
    onehot = jnp.where(hit, 1.0, 0.0).astype(BF16)
    order = lax.broadcasted_iota(jnp.int32, (count, count), 0) < lax.broadcasted_iota(
        jnp.int32, (count, count), 1
    )
    before = dot(onehot, jnp.where(order, 1.0, 0.0).astype(BF16))
    bases = bases_ref[...].astype(F32)
    place = before + jnp.where(before < TILE, bases[:, 0:1], bases[:, 1:2])
    slot = jnp.sum(jnp.where(hit, place, 0.0), axis=0, keepdims=True)
    slot_ref[...] = slot.astype(jnp.int32)

    def fill(index, carry):
        here = pl.multiple_of(index * BLK, BLK)
        wanted = lax.broadcasted_iota(jnp.int32, (BLK, count), 0) + here
        pick = jnp.where(wanted == slot_ref[...], 1.0, 0.0).astype(BF16)
        out_ref[pl.ds(here, BLK), :] = dot(pick, rows_ref[...]).astype(BF16)
        return carry

    lax.fori_loop(0, out_ref.shape[0] // BLK, fill, 0)


def pack_rows(routes, bases, rows, slots, name):
    count, width = rows.shape
    return pl.pallas_call(
        slot_kernel,
        out_shape=jax.ShapeDtypeStruct((slots, width), BF16),
        in_specs=[pl.BlockSpec(memory_space=pltpu.VMEM)] * 3,
        out_specs=pl.BlockSpec(memory_space=pltpu.VMEM),
        scratch_shapes=[pltpu.VMEM((1, count), jnp.int32)],
        compiler_params=pltpu.CompilerParams(vmem_limit_bytes=32 * 1024 * 1024),
        cost_estimate=pl.CostEstimate(
            flops=3_000_000_000, bytes_accessed=2_000_000, transcendentals=0
        ),
        name=name,
    )(routes, bases, rows)


def project_kernel(rows_ref, weights_ref, out_ref):
    parts, blocks = rows_ref.shape[:2]
    width = out_ref.shape[3]
    slots = blocks * TILE
    upper = lax.broadcasted_iota(jnp.int32, (slots, 1), 0) % TILE < TILE // 2

    def tile_rows(tile):
        return jnp.concatenate(
            [rows_ref[m, :, tile].reshape(slots, -1) for m in range(parts)], axis=1
        )

    ends = tile_rows(2)
    none = jnp.zeros_like(ends)
    mixed = None
    for local in range(2):
        end = jnp.where(upper, ends, none) if local == 0 else jnp.where(upper, none, ends)
        rows = jnp.concatenate([tile_rows(local), end], axis=0)
        value = dot(rows, weights_ref[local])
        out_ref[:, local] = value[:slots].astype(BF16).reshape(blocks, TILE, width)
        mixed = value[slots:] if mixed is None else mixed + value[slots:]
    out_ref[:, 2] = mixed.astype(BF16).reshape(blocks, TILE, width)


def project_rows(rows, weights):
    parts, blocks, _, _, hidden_part = rows.shape
    width = weights.shape[2]
    step = 16
    return pl.pallas_call(
        project_kernel,
        out_shape=jax.ShapeDtypeStruct((blocks, HELD, TILE, width), BF16),
        grid=(blocks // step,),
        in_specs=[
            pl.BlockSpec((parts, step, HELD, TILE, hidden_part), lambda i: (0, i, 0, 0, 0)),
            pl.BlockSpec(weights.shape, lambda i: (0, 0, 0)),
        ],
        out_specs=pl.BlockSpec((step, HELD, TILE, width), lambda i: (i, 0, 0, 0)),
        compiler_params=pltpu.CompilerParams(vmem_limit_bytes=VMEM_GRANT),
        cost_estimate=pl.CostEstimate(
            flops=4_000_000_000, bytes_accessed=10_000_000, transcendentals=0
        ),
        name="project_rows",
    )(rows, weights)


def regroup_kernel(members_ref, held_ref, out_ref):
    groups = out_ref.shape[0]
    first = pl.program_id(0) * groups
    width = held_ref.shape[3]
    blocks = width // LANES
    upper = lax.broadcasted_iota(jnp.int32, (TILE, width), 0) < TILE // 2
    upper_block = upper[:, :LANES]

    def lanes(value, block):
        return value[:, block * LANES : (block + 1) * LANES]

    def regroup(index, carry):
        ends = []
        for layer in range(GMAX):
            member = members_ref[(first + index) * GMAX + layer]
            holder, local = member // 2, member % 2
            rows = held_ref[holder, local]
            for block in range(blocks):
                out_ref[index, KEPT * block + layer] = lanes(rows, block)
            end = held_ref[holder, 2].astype(F32)
            turned = pltpu.roll(end, TILE // 2, 0)
            ends.append(jnp.where(local == layer % 2, end, turned))
        pair = jnp.where(upper, ends[0], ends[1]).astype(BF16)
        for block in range(blocks):
            out_ref[index, KEPT * block + GMAX] = lanes(pair, block)
        last = pltpu.roll(ends[2], TILE // 2, 0)
        for block in range(KEPT):
            low = lanes(last, block + KEPT) if block + KEPT < blocks else 0.0
            value = jnp.where(upper_block, lanes(ends[2], block), low)
            out_ref[index, KEPT * blocks + block] = value.astype(BF16)
        return carry

    lax.fori_loop(0, groups, regroup, 0)


def regroup_rows(held, members):
    group_count, _, _, width = held.shape
    part = group_count // 4
    tiles = KEPT * (width // LANES) + KEPT
    return pl.pallas_call(
        regroup_kernel,
        out_shape=jax.ShapeDtypeStruct((group_count, tiles, TILE, LANES), BF16),
        grid_spec=pltpu.PrefetchScalarGridSpec(
            num_scalar_prefetch=1,
            grid=(4,),
            in_specs=[pl.BlockSpec(held.shape, lambda i, m: (0, 0, 0, 0))],
            out_specs=pl.BlockSpec((part, tiles, TILE, LANES), lambda i, m: (i, 0, 0, 0)),
        ),
        compiler_params=pltpu.CompilerParams(vmem_limit_bytes=VMEM_GRANT),
        cost_estimate=pl.CostEstimate(
            flops=0, bytes_accessed=7_500_000, transcendentals=0
        ),
        name="regroup_rows",
    )(members, held)


def invert_kernel(rows_ref, after_ref, inverse_ref, turned_ref, sys_ref):
    del after_ref
    count, blocks = rows_ref.shape[:2]
    width = count * BLK
    kept = blocks * KEPT * TILE
    ends = blocks * TILE
    diag = lax.broadcasted_iota(jnp.int32, (BLK, BLK), 0) == lax.broadcasted_iota(
        jnp.int32, (BLK, BLK), 1
    )

    def span(index):
        return pl.ds(pl.multiple_of(index * BLK, BLK), BLK)

    def turn(i, carry):
        turned_ref[span(i), :kept] = rows_ref[i, :, :KEPT].reshape(kept, BLK).T
        last = rows_ref[i, :, KEPT].reshape(ends, BLK)
        turned_ref[span(i), kept:] = last.T
        return carry

    lax.fori_loop(0, count, turn, 0)

    def gram_block(index, carry):
        i, j = index // count, index % count
        value = dot(turned_ref[span(i), :kept], rows_ref[j, :, :KEPT].reshape(kept, BLK))
        last = rows_ref[j, :, KEPT].reshape(ends, BLK)
        sys_ref[span(i), span(j)] = value + dot(turned_ref[span(i), kept:], last)
        return carry

    lax.fori_loop(0, count * count, gram_block, 0)
    trace = jnp.float32(0)
    for i in range(count):
        here = slice(i * BLK, (i + 1) * BLK)
        trace = trace + jnp.sum(jnp.where(diag, sys_ref[here, here], 0.0))
    ridge = damping * trace / width + epsilon
    for i in range(count):
        here = slice(i * BLK, (i + 1) * BLK)
        sys_ref[here, here] = sys_ref[here, here] + jnp.where(diag, ridge, 0.0)

    def sweep(k, carry):
        inverse = block_inverse(sys_ref[span(k), span(k)], ridge)
        inverse_parts = thirds(inverse)
        panel = dot6(inverse_parts, thirds(sys_ref[span(k), :]))
        panel_parts = thirds(panel)

        def eliminate(i, inner):
            @pl.when(i != k)
            def _():
                left = thirds(sys_ref[span(i), span(k)])
                sys_ref[span(i), :] = sys_ref[span(i), :] - dot6(left, panel_parts)
                sys_ref[span(i), span(k)] = dot6(left, inverse_parts)

            return inner

        lax.fori_loop(0, count, eliminate, 0)
        sys_ref[span(k), :] = panel
        sys_ref[span(k), span(k)] = -inverse
        return carry

    lax.fori_loop(0, count, sweep, 0)

    def split(i, carry):
        high, low = halves(-sys_ref[span(i), :])
        inverse_ref[span(i), :width] = high
        inverse_ref[span(i), width : 2 * width] = high
        inverse_ref[span(i), 2 * width :] = low
        return carry

    lax.fori_loop(0, count, split, 0)


def invert_gram(rows, after):
    count, blocks, _, _, _ = rows.shape
    width = count * BLK
    slots = blocks * TILE * OWNED
    return pl.pallas_call(
        invert_kernel,
        out_shape=(
            jax.ShapeDtypeStruct((width, 3 * width), BF16),
            jax.ShapeDtypeStruct((width, slots), BF16),
        ),
        in_specs=[
            pl.BlockSpec(memory_space=pltpu.VMEM),
            pl.BlockSpec(memory_space=pl.ANY),
        ],
        out_specs=[pl.BlockSpec(memory_space=pltpu.VMEM)] * 2,
        scratch_shapes=[pltpu.VMEM((width, width), F32)],
        compiler_params=pltpu.CompilerParams(vmem_limit_bytes=VMEM_GRANT),
        cost_estimate=pl.CostEstimate(
            flops=60_000_000_000, bytes_accessed=16_000_000, transcendentals=0
        ),
        name="invert_gram",
    )(rows, after)


def merge_kernel(
    packed_hbm, turned_hbm, inverse_hbm, out_ref, packed_ref, turned_ref, inverse_ref, rows_ref, partial_ref, sems
):
    groups = packed_ref.shape[0]
    size, width = out_ref.shape
    blocks = width // LANES
    kept = groups * KEPT * TILE
    ends = groups * TILE
    step = 2 * BLK
    pairs = ((packed_hbm, packed_ref), (turned_hbm, turned_ref), (inverse_hbm, inverse_ref))
    copies = [
        pltpu.make_async_copy(source, target, sems.at[index])
        for index, (source, target) in enumerate(pairs)
    ]
    for copy in copies:
        copy.start()
    copies[0].wait()
    for block in range(blocks):
        lanes = slice(block * LANES, (block + 1) * LANES)
        rows = packed_ref[:, KEPT * block : KEPT * block + KEPT]
        rows_ref[:kept, lanes] = rows.reshape(kept, LANES)
        last = packed_ref[:, KEPT * blocks + block % KEPT].reshape(ends, LANES)
        if block >= KEPT:
            last = pltpu.roll(last.astype(F32), ends - TILE // 2, 0).astype(BF16)
        rows_ref[kept:, lanes] = last
    copies[1].wait()

    def span(index, offset):
        return pl.ds(pl.multiple_of(index * step + offset, step), step)

    def gather(i, carry):
        high, low = halves(dot(turned_ref[span(i, 0), :], rows_ref[...]))
        partial_ref[span(i, 0), :] = high
        partial_ref[span(i, size), :] = low
        partial_ref[span(i, 2 * size), :] = high
        return carry

    lax.fori_loop(0, size // step, gather, 0)
    copies[2].wait()

    def strip(i, carry):
        value = dot(inverse_ref[span(i, 0), :], partial_ref[...])
        out_ref[span(i, 0), :] = value.astype(BF16)
        return carry

    lax.fori_loop(0, size // step, strip, 0)


def merge_rows(packed, turned, inverse):
    size, slots = turned.shape
    width = (packed.shape[1] // KEPT - 1) * LANES
    operands = (packed, turned, inverse)
    return pl.pallas_call(
        merge_kernel,
        out_shape=jax.ShapeDtypeStruct((size, width), BF16),
        in_specs=[pl.BlockSpec(memory_space=pl.ANY)] * 3,
        out_specs=pl.BlockSpec(memory_space=pltpu.VMEM),
        scratch_shapes=[pltpu.VMEM(operand.shape, BF16) for operand in operands]
        + [
            pltpu.VMEM((slots, width), BF16),
            pltpu.VMEM((3 * size, width), BF16),
            pltpu.SemaphoreType.DMA((3,)),
        ],
        compiler_params=pltpu.CompilerParams(vmem_limit_bytes=VMEM_GRANT),
        cost_estimate=pl.CostEstimate(
            flops=10_300_000_000, bytes_accessed=16_000_000, transcendentals=0
        ),
        name="merge_rows",
    )(*operands)


def member_places(merge_group, group_count):
    experts = merge_group.shape[0]
    index = jnp.arange(experts, dtype=jnp.int32)
    earlier = index[None, :] < index[:, None]
    rank = jnp.sum(
        (merge_group[:, None] == merge_group[None, :]) & earlier, axis=1, dtype=jnp.int32
    )
    place = merge_group * GMAX + rank
    wanted = jnp.arange(group_count * GMAX, dtype=jnp.int32)
    members = jnp.sum(jnp.where(place[None, :] == wanted[:, None], index[None, :], 0), axis=1)
    chunk = merge_group * (OWNED * TILE)
    bases = [chunk + rank * TILE, chunk + GMAX * TILE + rank * (TILE // 2) - TILE]
    return members, jnp.stack(bases, axis=1)


def exchange(rows):
    return lax.all_to_all(rows, "expert", split_axis=0, concat_axis=0, tiled=True)


def on_device(routes, routed_hidden, down_proj, merge_group):
    group_count = lax.axis_size("expert")
    parts = lax.axis_size("mp")
    full_width, out_part = down_proj.shape[1:]
    tok_count, top_count, hidden_part = routed_hidden.shape
    row_count = tok_count * top_count
    experts = merge_group.shape[0]

    rows = routed_hidden.reshape(row_count, hidden_part)
    targets = routes.reshape(1, row_count)
    index = jnp.arange(experts, dtype=jnp.int32)
    chunk, local = index // 2 * (HELD * TILE), index % 2
    held_bases = jnp.stack(
        [chunk + local * TILE, chunk + 2 * TILE + local * (TILE // 2) - TILE], axis=1
    )
    members, owned_bases = member_places(merge_group, group_count)

    to_holder = pack_rows(
        targets, held_bases, rows, group_count * HELD * TILE, "pack_held"
    ).reshape(group_count, HELD * TILE, hidden_part)
    to_owner = pack_rows(
        targets, owned_bases, rows, group_count * OWNED * TILE, "pack_owned"
    ).reshape(group_count, OWNED * TILE, hidden_part)
    at_holder = exchange(to_holder)
    at_holder, to_owner = lax.optimization_barrier((at_holder, to_owner))
    held = lax.all_gather(at_holder, "mp", axis=0)
    at_owner = exchange(to_owner)

    projected = project_rows(
        held.reshape(parts, group_count, HELD, TILE, hidden_part), down_proj
    )
    at_owner, projected = lax.optimization_barrier((at_owner, projected))
    home = exchange(projected.reshape(group_count, HELD * TILE, out_part))
    owned = lax.all_gather(at_owner, "mp", axis=0)
    regrouped = regroup_rows(home.reshape(group_count, HELD, TILE, out_part), members)
    arrived = exchange(regrouped)

    inverse, turned = invert_gram(
        owned.reshape(parts, group_count, OWNED, TILE, hidden_part), regrouped
    )
    merged = merge_rows(arrived, turned, inverse)
    return merged.reshape(1, full_width, out_part)


def solution(mesh):
    return jax.shard_map(
        on_device,
        mesh=mesh,
        in_specs=(P("expert", None), P("expert", None, "mp"), P("expert", None, "mp"), P()),
        out_specs=P("expert", None, "mp"),
        check_vma=False,
    )
```

```python
import jax
import jax.numpy as jnp
from jax import lax
from jax.experimental import pallas as pl
from jax.experimental.pallas import tpu as pltpu
from jax.sharding import PartitionSpec as P

GMAX = 3
BLK = 256
damping = 0.1
epsilon = 1e-05
F32 = jnp.float32
BF16 = jnp.bfloat16


def sweep_counts():
    gaps, delta = [], 1e-3
    for _ in range(16):
        gaps.append(1.0 - delta)
        if 2.0 * delta / (1.0 + delta) > 2.0 - 2.0 / GAIN_MAX:
            delta = (1.0 - (1.0 - delta) / GAIN_MAX) ** 0.5
        else:
            delta = (2.0 * delta / (1.0 + delta)) ** 0.5
    return gaps


GAIN_MAX = 1.85
NEWTON_GAPS = sweep_counts()


def halves(value):
    high = value.astype(BF16)
    return high, (value - high.astype(F32)).astype(BF16)


def dot(a, b):
    return jnp.dot(a, b, preferred_element_type=F32)


def dot3(a, b):
    (ah, al), (bh, bl) = a, b
    return dot(ah, bh) + (dot(ah, bl) + dot(al, bh))


def thirds(value):
    high = value.astype(BF16)
    rest = value - high.astype(F32)
    mid = rest.astype(BF16)
    return high, mid, (rest - mid.astype(F32)).astype(BF16)


def dot6(a, b):
    (ah, am, al), (bh, bm, bl) = a, b
    small = dot(am, bm) + (dot(ah, bl) + dot(al, bh))
    return dot(ah, bh) + (dot(ah, bm) + dot(am, bh) + small)


def block_inverse(block, lower):
    size = block.shape[0]
    upper = jnp.max(jnp.sum(jnp.abs(block), axis=1, keepdims=True))
    gap = 2.0 * lower / (lower + upper)
    steps = jnp.int32(0)
    for edge in NEWTON_GAPS:
        steps = steps + (gap < edge).astype(jnp.int32)
    rows = lax.broadcasted_iota(jnp.int32, (size, size), 0)
    cols = lax.broadcasted_iota(jnp.int32, (size, size), 1)
    total = jnp.full((1, size), lower + upper, F32)
    start = jnp.where(rows == cols, 2.0 / total, 0.0)
    block_parts = thirds(block)

    def step(_, carry):
        guess, delta = carry
        parts = halves(guess)
        image = dot3(block_parts[:2], parts)
        gain = jnp.minimum(2.0 / (2.0 - delta * delta), GAIN_MAX)
        guess = gain * (2.0 * guess - dot3(parts, halves(image)))
        return guess, 1.0 - gain * (1.0 - delta * delta)

    guess, _ = lax.fori_loop(0, steps, step, (start, 1.0 - 2.0 * lower / total))
    parts = thirds(guess)
    return 2.0 * guess - dot6(parts, thirds(dot6(block_parts, parts)))


TILE = 8
HELD = 3
OWNED = 5
KEPT = 4
LANES = 128
UNROLL = 4
PROJECT_STEP = 32
VMEM_GRANT = 58 * 1024 * 1024


def slot_kernel(routes_ref, bases_ref, rows_ref, out_ref, slot_ref):
    experts = bases_ref.shape[0]
    count = routes_ref.shape[1]
    hit = lax.broadcasted_iota(jnp.int32, (experts, count), 0) == routes_ref[...]
    onehot = jnp.where(hit, 1.0, 0.0).astype(BF16)
    order = lax.broadcasted_iota(jnp.int32, (count, count), 0) < lax.broadcasted_iota(
        jnp.int32, (count, count), 1
    )
    before = dot(onehot, jnp.where(order, 1.0, 0.0).astype(BF16))
    bases = bases_ref[...].astype(F32)
    place = before + jnp.where(before < TILE, bases[:, 0:1], bases[:, 1:2])
    slot = jnp.sum(jnp.where(hit, place, 0.0), axis=0, keepdims=True)
    slot_ref[...] = slot.astype(jnp.int32)

    def fill(index, carry):
        here = pl.multiple_of(index * BLK, BLK)
        wanted = lax.broadcasted_iota(jnp.int32, (BLK, count), 0) + here
        pick = jnp.where(wanted == slot_ref[...], 1.0, 0.0).astype(BF16)
        out_ref[pl.ds(here, BLK), :] = dot(pick, rows_ref[...]).astype(BF16)
        return carry

    lax.fori_loop(0, out_ref.shape[0] // BLK, fill, 0)


def pack_rows(routes, bases, rows, slots, name):
    count, width = rows.shape
    return pl.pallas_call(
        slot_kernel,
        out_shape=jax.ShapeDtypeStruct((slots, width), BF16),
        in_specs=[pl.BlockSpec(memory_space=pltpu.VMEM)] * 3,
        out_specs=pl.BlockSpec(memory_space=pltpu.VMEM),
        scratch_shapes=[pltpu.VMEM((1, count), jnp.int32)],
        compiler_params=pltpu.CompilerParams(vmem_limit_bytes=32 * 1024 * 1024),
        cost_estimate=pl.CostEstimate(
            flops=3_000_000_000, bytes_accessed=2_000_000, transcendentals=0
        ),
        name=name,
    )(routes, bases, rows)


def project_kernel(rows_ref, weights_ref, out_ref):
    parts, blocks = rows_ref.shape[:2]
    width = out_ref.shape[3]
    slots = blocks * TILE
    upper = lax.broadcasted_iota(jnp.int32, (slots, 1), 0) % TILE < TILE // 2

    def tile_rows(tile):
        return jnp.concatenate(
            [rows_ref[m, :, tile].reshape(slots, -1) for m in range(parts)], axis=1
        )

    ends = tile_rows(2)
    none = jnp.zeros_like(ends)
    mixed = None
    for local in range(2):
        end = jnp.where(upper, ends, none) if local == 0 else jnp.where(upper, none, ends)
        rows = jnp.concatenate([tile_rows(local), end], axis=0)
        value = dot(rows, weights_ref[local])
        out_ref[:, local] = value[:slots].astype(BF16).reshape(blocks, TILE, width)
        mixed = value[slots:] if mixed is None else mixed + value[slots:]
    out_ref[:, 2] = mixed.astype(BF16).reshape(blocks, TILE, width)


def project_rows(rows, weights):
    parts, blocks, _, _, hidden_part = rows.shape
    width = weights.shape[2]
    step = PROJECT_STEP
    return pl.pallas_call(
        project_kernel,
        out_shape=jax.ShapeDtypeStruct((blocks, HELD, TILE, width), BF16),
        grid=(blocks // step,),
        in_specs=[
            pl.BlockSpec((parts, step, HELD, TILE, hidden_part), lambda i: (0, i, 0, 0, 0)),
            pl.BlockSpec(weights.shape, lambda i: (0, 0, 0)),
        ],
        out_specs=pl.BlockSpec((step, HELD, TILE, width), lambda i: (i, 0, 0, 0)),
        compiler_params=pltpu.CompilerParams(vmem_limit_bytes=VMEM_GRANT),
        cost_estimate=pl.CostEstimate(
            flops=4_000_000_000, bytes_accessed=10_000_000, transcendentals=0
        ),
        name="project_rows",
    )(rows, weights)


def regroup_kernel(members_ref, held_ref, out_hbm, out_ref, sems):
    parts, groups = out_ref.shape[:2]
    width = held_ref.shape[3]
    blocks = width // LANES
    upper = lax.broadcasted_iota(jnp.int32, (TILE, width), 0) < TILE // 2
    upper_block = upper[:, :LANES]

    def lanes(value, block):
        return value[:, block * LANES : (block + 1) * LANES]

    def regroup(part, index):
        ends = []
        for layer in range(GMAX):
            member = members_ref[(part * groups + index) * GMAX + layer]
            holder, local = member >> 1, member & 1
            rows = held_ref[holder, local]
            for block in range(blocks):
                out_ref[part, index, KEPT * block + layer] = lanes(rows, block)
            end = held_ref[holder, 2].astype(F32)
            turned = pltpu.roll(end, TILE // 2, 0)
            ends.append(jnp.where(local == layer % 2, end, turned))
        pair = jnp.where(upper, ends[0], ends[1]).astype(BF16)
        for block in range(blocks):
            out_ref[part, index, KEPT * block + GMAX] = lanes(pair, block)
        last = pltpu.roll(ends[2], TILE // 2, 0)
        for block in range(KEPT):
            low = lanes(last, block + KEPT) if block + KEPT < blocks else 0.0
            value = jnp.where(upper_block, lanes(ends[2], block), low)
            out_ref[part, index, KEPT * blocks + block] = value.astype(BF16)

    copies = []
    for part in range(parts):

        def several(index, carry, part=part):
            for k in range(UNROLL):
                regroup(part, index * UNROLL + k)
            return carry

        lax.fori_loop(0, groups // UNROLL, several, 0)
        copies.append(
            pltpu.make_async_copy(
                out_ref.at[part], out_hbm.at[pl.ds(part * groups, groups)], sems.at[part]
            )
        )
        copies[-1].start()
    for copy in copies:
        copy.wait()


def regroup_rows(held, members):
    group_count, _, _, width = held.shape
    parts = 4
    tiles = KEPT * (width // LANES) + KEPT
    return pl.pallas_call(
        regroup_kernel,
        out_shape=jax.ShapeDtypeStruct((group_count, tiles, TILE, LANES), BF16),
        in_specs=[
            pl.BlockSpec(memory_space=pltpu.SMEM),
            pl.BlockSpec(memory_space=pltpu.VMEM),
        ],
        out_specs=pl.BlockSpec(memory_space=pltpu.HBM),
        scratch_shapes=[
            pltpu.VMEM((parts, group_count // parts, tiles, TILE, LANES), BF16),
            pltpu.SemaphoreType.DMA((parts,)),
        ],
        compiler_params=pltpu.CompilerParams(vmem_limit_bytes=16 * 1024 * 1024),
        cost_estimate=pl.CostEstimate(
            flops=0, bytes_accessed=7_500_000, transcendentals=0
        ),
        name="regroup_rows",
    )(members, held)


def invert_kernel(rows_ref, after_ref, maps_ref, turned_ref, sys_ref):
    del after_ref
    count, blocks = rows_ref.shape[:2]
    width = count * BLK
    kept = blocks * KEPT * TILE
    ends = blocks * TILE
    diag = lax.broadcasted_iota(jnp.int32, (BLK, BLK), 0) == lax.broadcasted_iota(
        jnp.int32, (BLK, BLK), 1
    )

    def span(index):
        return pl.ds(pl.multiple_of(index * BLK, BLK), BLK)

    def turn(i, carry):
        turned_ref[span(i), :kept] = rows_ref[i, :, :KEPT].reshape(kept, BLK).T
        last = rows_ref[i, :, KEPT].reshape(ends, BLK)
        turned_ref[span(i), kept:] = last.T
        return carry

    lax.fori_loop(0, count, turn, 0)

    def gram_block(index, carry):
        i, j = index // count, index % count
        value = dot(turned_ref[span(i), :kept], rows_ref[j, :, :KEPT].reshape(kept, BLK))
        last = rows_ref[j, :, KEPT].reshape(ends, BLK)
        sys_ref[span(i), span(j)] = value + dot(turned_ref[span(i), kept:], last)
        return carry

    lax.fori_loop(0, count * count, gram_block, 0)
    trace = jnp.float32(0)
    for i in range(count):
        here = slice(i * BLK, (i + 1) * BLK)
        trace = trace + jnp.sum(jnp.where(diag, sys_ref[here, here], 0.0))
    ridge = damping * trace / width + epsilon
    for i in range(count):
        here = slice(i * BLK, (i + 1) * BLK)
        sys_ref[here, here] = sys_ref[here, here] + jnp.where(diag, ridge, 0.0)

    def sweep(k, carry):
        inverse = block_inverse(sys_ref[span(k), span(k)], ridge)
        inverse_parts = thirds(inverse)
        panel = dot6(inverse_parts, thirds(sys_ref[span(k), :]))
        panel_parts = thirds(panel)

        def eliminate(i, inner):
            @pl.when(i != k)
            def _():
                left = thirds(sys_ref[span(i), span(k)])
                sys_ref[span(i), :] = sys_ref[span(i), :] - dot6(left, panel_parts)
                sys_ref[span(i), span(k)] = dot6(left, inverse_parts)

            return inner

        lax.fori_loop(0, count, eliminate, 0)
        sys_ref[span(k), :] = panel
        sys_ref[span(k), span(k)] = -inverse
        return carry

    lax.fori_loop(0, count, sweep, 0)

    def map_block(index, carry):
        i, j = index // strips, index % strips
        here = pl.ds(pl.multiple_of(j * strip, strip), strip)
        both = jnp.concatenate(halves(-sys_ref[span(i), :]), axis=0)
        value = dot(both, turned_ref[:, here])
        high, low = halves(value[:BLK] + value[BLK:])
        maps_ref[span(2 * i), here] = high
        maps_ref[span(2 * i + 1), here] = low
        return carry

    strip = 2 * BLK
    strips = (kept + ends) // strip
    lax.fori_loop(0, count * strips, map_block, 0)


def invert_gram(rows, after):
    count, blocks, _, _, _ = rows.shape
    width = count * BLK
    slots = blocks * TILE * OWNED
    return pl.pallas_call(
        invert_kernel,
        out_shape=jax.ShapeDtypeStruct((2 * width, slots), BF16),
        in_specs=[
            pl.BlockSpec(memory_space=pltpu.VMEM),
            pl.BlockSpec(memory_space=pl.ANY),
        ],
        out_specs=pl.BlockSpec(memory_space=pltpu.VMEM),
        scratch_shapes=[pltpu.VMEM((width, slots), BF16), pltpu.VMEM((width, width), F32)],
        compiler_params=pltpu.CompilerParams(vmem_limit_bytes=VMEM_GRANT),
        cost_estimate=pl.CostEstimate(
            flops=60_000_000_000, bytes_accessed=16_000_000, transcendentals=0
        ),
        name="invert_gram",
    )(rows, after)


def merge_kernel(packed_hbm, maps_hbm, out_ref, packed_ref, maps_ref, rows_ref, sems):
    groups = packed_ref.shape[0]
    size, width = out_ref.shape
    blocks = width // LANES
    kept = groups * KEPT * TILE
    ends = groups * TILE
    first = pltpu.make_async_copy(packed_hbm, packed_ref, sems.at[0])
    first.start()
    copies = []
    for index in range(size // BLK):
        here = slice(2 * index * BLK, 2 * (index + 1) * BLK)
        copies.append(
            pltpu.make_async_copy(maps_hbm.at[here], maps_ref.at[here], sems.at[index + 1])
        )
        copies[-1].start()
    first.wait()
    for block in range(blocks):
        lanes = slice(block * LANES, (block + 1) * LANES)
        rows = packed_ref[:, KEPT * block : KEPT * block + KEPT]
        rows_ref[:kept, lanes] = rows.reshape(kept, LANES)
        last = packed_ref[:, KEPT * blocks + block % KEPT].reshape(ends, LANES)
        if block >= KEPT:
            last = pltpu.roll(last.astype(F32), ends - TILE // 2, 0).astype(BF16)
        rows_ref[kept:, lanes] = last
    for index, copy in enumerate(copies):
        copy.wait()
        value = dot(maps_ref[2 * index * BLK : 2 * (index + 1) * BLK], rows_ref[...])
        here = slice(index * BLK, (index + 1) * BLK)
        out_ref[here] = (value[:BLK] + value[BLK:]).astype(BF16)


def merge_rows(packed, maps):
    size, slots = maps.shape
    width = (packed.shape[1] // KEPT - 1) * LANES
    return pl.pallas_call(
        merge_kernel,
        out_shape=jax.ShapeDtypeStruct((size // 2, width), BF16),
        in_specs=[pl.BlockSpec(memory_space=pl.ANY)] * 2,
        out_specs=pl.BlockSpec(memory_space=pltpu.VMEM),
        scratch_shapes=[
            pltpu.VMEM(packed.shape, BF16),
            pltpu.VMEM(maps.shape, BF16),
            pltpu.VMEM((slots, width), BF16),
            pltpu.SemaphoreType.DMA((1 + size // (2 * BLK),)),
        ],
        compiler_params=pltpu.CompilerParams(vmem_limit_bytes=VMEM_GRANT),
        cost_estimate=pl.CostEstimate(
            flops=9_400_000_000, bytes_accessed=16_000_000, transcendentals=0
        ),
        name="merge_rows",
    )(packed, maps)


def member_places(merge_group, group_count):
    experts = merge_group.shape[0]
    index = jnp.arange(experts, dtype=jnp.int32)
    earlier = index[None, :] < index[:, None]
    rank = jnp.sum(
        (merge_group[:, None] == merge_group[None, :]) & earlier, axis=1, dtype=jnp.int32
    )
    place = merge_group * GMAX + rank
    wanted = jnp.arange(group_count * GMAX, dtype=jnp.int32)
    members = jnp.sum(jnp.where(place[None, :] == wanted[:, None], index[None, :], 0), axis=1)
    chunk = merge_group * (OWNED * TILE)
    bases = [chunk + rank * TILE, chunk + GMAX * TILE + rank * (TILE // 2) - TILE]
    return members, jnp.stack(bases, axis=1)


def exchange(rows):
    return lax.all_to_all(rows, "expert", split_axis=0, concat_axis=0, tiled=True)


def on_device(routes, routed_hidden, down_proj, merge_group):
    group_count = lax.axis_size("expert")
    parts = lax.axis_size("mp")
    full_width, out_part = down_proj.shape[1:]
    tok_count, top_count, hidden_part = routed_hidden.shape
    row_count = tok_count * top_count
    experts = merge_group.shape[0]

    rows = routed_hidden.reshape(row_count, hidden_part)
    targets = routes.reshape(1, row_count)
    index = jnp.arange(experts, dtype=jnp.int32)
    chunk, local = index // 2 * (HELD * TILE), index % 2
    held_bases = jnp.stack(
        [chunk + local * TILE, chunk + 2 * TILE + local * (TILE // 2) - TILE], axis=1
    )
    members, owned_bases = member_places(merge_group, group_count)

    to_holder = pack_rows(
        targets, held_bases, rows, group_count * HELD * TILE, "pack_held"
    ).reshape(group_count, HELD * TILE, hidden_part)
    to_owner = pack_rows(
        targets, owned_bases, rows, group_count * OWNED * TILE, "pack_owned"
    ).reshape(group_count, OWNED * TILE, hidden_part)
    at_holder = exchange(to_holder)
    at_holder, to_owner = lax.optimization_barrier((at_holder, to_owner))
    held = lax.all_gather(at_holder, "mp", axis=0)
    at_owner = exchange(to_owner)

    projected = project_rows(
        held.reshape(parts, group_count, HELD, TILE, hidden_part), down_proj
    )
    at_owner, projected = lax.optimization_barrier((at_owner, projected))
    home = exchange(projected.reshape(group_count, HELD * TILE, out_part))
    owned = lax.all_gather(at_owner, "mp", axis=0)
    regrouped = regroup_rows(home.reshape(group_count, HELD, TILE, out_part), members)
    arrived = exchange(regrouped)

    maps = invert_gram(
        owned.reshape(parts, group_count, OWNED, TILE, hidden_part), regrouped
    )
    merged = merge_rows(arrived, maps)
    return merged.reshape(1, full_width, out_part)


def solution(mesh):
    return jax.shard_map(
        on_device,
        mesh=mesh,
        in_specs=(P("expert", None), P("expert", None, "mp"), P("expert", None, "mp"), P()),
        out_specs=P("expert", None, "mp"),
        check_vma=False,
    )
```

```python
import jax
import jax.numpy as jnp
from jax import lax
from jax.experimental import pallas as pl
from jax.experimental.pallas import tpu as pltpu
from jax.sharding import PartitionSpec as P

GMAX = 3
BLK = 256
damping = 0.1
epsilon = 1e-05
F32 = jnp.float32
BF16 = jnp.bfloat16


def sweep_counts():
    gaps, delta = [], 1e-3
    for _ in range(16):
        gaps.append(1.0 - delta)
        if 2.0 * delta / (1.0 + delta) > 2.0 - 2.0 / GAIN_MAX:
            delta = (1.0 - (1.0 - delta) / GAIN_MAX) ** 0.5
        else:
            delta = (2.0 * delta / (1.0 + delta)) ** 0.5
    return gaps


GAIN_MAX = 1.85
NEWTON_GAPS = sweep_counts()


def halves(value):
    high = value.astype(BF16)
    return high, (value - high.astype(F32)).astype(BF16)


def dot(a, b):
    return jnp.dot(a, b, preferred_element_type=F32)


def dot3(a, b):
    (ah, al), (bh, bl) = a, b
    return dot(ah, bh) + (dot(ah, bl) + dot(al, bh))


def thirds(value):
    high = value.astype(BF16)
    rest = value - high.astype(F32)
    mid = rest.astype(BF16)
    return high, mid, (rest - mid.astype(F32)).astype(BF16)


def dot6(a, b):
    (ah, am, al), (bh, bm, bl) = a, b
    small = dot(am, bm) + (dot(ah, bl) + dot(al, bh))
    return dot(ah, bh) + (dot(ah, bm) + dot(am, bh) + small)


def block_inverse(block, lower):
    size = block.shape[0]
    upper = jnp.max(jnp.sum(jnp.abs(block), axis=1, keepdims=True))
    gap = 2.0 * lower / (lower + upper)
    steps = jnp.int32(0)
    for edge in NEWTON_GAPS:
        steps = steps + (gap < edge).astype(jnp.int32)
    rows = lax.broadcasted_iota(jnp.int32, (size, size), 0)
    cols = lax.broadcasted_iota(jnp.int32, (size, size), 1)
    total = jnp.full((1, size), lower + upper, F32)
    start = jnp.where(rows == cols, 2.0 / total, 0.0)
    block_parts = thirds(block)

    def step(_, carry):
        guess, delta = carry
        parts = halves(guess)
        image = dot3(block_parts[:2], parts)
        gain = jnp.minimum(2.0 / (2.0 - delta * delta), GAIN_MAX)
        guess = gain * (2.0 * guess - dot3(parts, halves(image)))
        return guess, 1.0 - gain * (1.0 - delta * delta)

    guess, _ = lax.fori_loop(0, steps, step, (start, 1.0 - 2.0 * lower / total))
    parts = thirds(guess)
    return 2.0 * guess - dot6(parts, thirds(dot6(block_parts, parts)))


TILE = 8
HELD = 3
OWNED = 5
KEPT = 4
LANES = 128
UNROLL = 4
PROJECT_PARTS = 2
VMEM_GRANT = 58 * 1024 * 1024


def slot_kernel(routes_ref, bases_ref, rows_hbm, out_ref, slot_ref, rows_ref, sem):
    copy = pltpu.make_async_copy(rows_hbm, rows_ref, sem)
    copy.start()
    experts = bases_ref.shape[0]
    count = routes_ref.shape[1]
    hit = lax.broadcasted_iota(jnp.int32, (experts, count), 0) == routes_ref[...]
    onehot = jnp.where(hit, 1.0, 0.0).astype(BF16)
    order = lax.broadcasted_iota(jnp.int32, (count, count), 0) < lax.broadcasted_iota(
        jnp.int32, (count, count), 1
    )
    before = dot(onehot, jnp.where(order, 1.0, 0.0).astype(BF16))
    bases = bases_ref[...].astype(F32)
    place = before + jnp.where(before < TILE, bases[:, 0:1], bases[:, 1:2])
    slot = jnp.sum(jnp.where(hit, place, 0.0), axis=0, keepdims=True)
    slot_ref[...] = slot.astype(jnp.int32)
    copy.wait()

    def fill(index, carry):
        here = pl.multiple_of(index * BLK, BLK)
        wanted = lax.broadcasted_iota(jnp.int32, (BLK, count), 0) + here
        pick = jnp.where(wanted == slot_ref[...], 1.0, 0.0).astype(BF16)
        out_ref[pl.ds(here, BLK), :] = dot(pick, rows_ref[...]).astype(BF16)
        return carry

    lax.fori_loop(0, out_ref.shape[0] // BLK, fill, 0)


def pack_rows(routes, bases, rows, slots, name):
    count, width = rows.shape
    return pl.pallas_call(
        slot_kernel,
        out_shape=jax.ShapeDtypeStruct((slots, width), BF16),
        in_specs=[pl.BlockSpec(memory_space=pltpu.VMEM)] * 2
        + [pl.BlockSpec(memory_space=pl.ANY)],
        out_specs=pl.BlockSpec(memory_space=pltpu.VMEM),
        scratch_shapes=[
            pltpu.VMEM((1, count), jnp.int32),
            pltpu.VMEM(rows.shape, BF16),
            pltpu.SemaphoreType.DMA,
        ],
        compiler_params=pltpu.CompilerParams(vmem_limit_bytes=VMEM_GRANT),
        cost_estimate=pl.CostEstimate(
            flops=3_000_000_000, bytes_accessed=2_000_000, transcendentals=0
        ),
        name=name,
    )(routes, bases, rows)


def project_kernel(
    rows_hbm, weights_hbm, out_hbm, rows_ref, weights_ref, out_ref, mixed_ref, row_sems, weight_sems, out_sems
):
    parts, blocks = rows_ref.shape[:2]
    width = out_ref.shape[3]
    locals_count = weights_ref.shape[0]
    step = blocks // PROJECT_PARTS
    slots = step * TILE
    upper = lax.broadcasted_iota(jnp.int32, (slots, 1), 0) % TILE < TILE // 2

    def load_rows(part):
        here = pl.ds(part * step, step)
        return pltpu.make_async_copy(
            rows_hbm.at[:, here], rows_ref.at[:, here], row_sems.at[part]
        )

    def load_weights(local):
        return pltpu.make_async_copy(
            weights_hbm.at[local], weights_ref.at[local], weight_sems.at[local]
        )

    loads = [load_rows(0), load_weights(0)]
    loads += [load_rows(part) for part in range(1, PROJECT_PARTS)]
    loads += [load_weights(local) for local in range(1, locals_count)]
    for load in loads:
        load.start()
    stores = []

    def store(part, tile):
        here = pl.ds(part * step, step)
        copy = pltpu.make_async_copy(
            out_ref.at[here, tile], out_hbm.at[here, tile], out_sems.at[part, tile]
        )
        copy.start()
        stores.append(copy)

    for local in range(locals_count):
        for part in range(PROJECT_PARTS):
            here = slice(part * step, (part + 1) * step)
            if local == 0:
                load_rows(part).wait()
            if part == 0:
                load_weights(local).wait()

            def tile_rows(tile, here=here):
                return jnp.concatenate(
                    [rows_ref[m, here, tile].reshape(slots, -1) for m in range(parts)], axis=1
                )

            ends = tile_rows(2)
            none = jnp.zeros_like(ends)
            end = jnp.where(upper, ends, none) if local == 0 else jnp.where(upper, none, ends)
            rows = jnp.concatenate([tile_rows(local), end], axis=0)
            value = dot(rows, weights_ref[local])
            out_ref[here, local] = value[:slots].astype(BF16).reshape(step, TILE, width)
            store(part, local)
            if local == 0:
                mixed_ref[part] = value[slots:]
            else:
                mixed = mixed_ref[part] + value[slots:]
                out_ref[here, 2] = mixed.astype(BF16).reshape(step, TILE, width)
                store(part, 2)
    for copy in stores:
        copy.wait()


def project_rows(rows, weights):
    parts, blocks, _, _, hidden_part = rows.shape
    width = weights.shape[2]
    shape = (blocks, HELD, TILE, width)
    return pl.pallas_call(
        project_kernel,
        out_shape=pltpu.HBM(shape, BF16),
        in_specs=[pl.BlockSpec(memory_space=pl.ANY)] * 2,
        out_specs=pl.BlockSpec(memory_space=pltpu.HBM),
        scratch_shapes=[
            pltpu.VMEM(rows.shape, BF16),
            pltpu.VMEM(weights.shape, BF16),
            pltpu.VMEM(shape, BF16),
            pltpu.VMEM((PROJECT_PARTS, blocks // PROJECT_PARTS * TILE, width), F32),
            pltpu.SemaphoreType.DMA((PROJECT_PARTS,)),
            pltpu.SemaphoreType.DMA((weights.shape[0],)),
            pltpu.SemaphoreType.DMA((PROJECT_PARTS, HELD)),
        ],
        compiler_params=pltpu.CompilerParams(vmem_limit_bytes=VMEM_GRANT),
        cost_estimate=pl.CostEstimate(
            flops=4_000_000_000, bytes_accessed=10_000_000, transcendentals=0
        ),
        name="project_rows",
    )(rows, weights)


def regroup_kernel(members_ref, held_ref, out_hbm, out_ref, sems):
    parts, groups = out_ref.shape[:2]
    width = held_ref.shape[3]
    blocks = width // LANES
    upper = lax.broadcasted_iota(jnp.int32, (TILE, width), 0) < TILE // 2
    upper_block = upper[:, :LANES]

    def lanes(value, block):
        return value[:, block * LANES : (block + 1) * LANES]

    def regroup(part, index):
        ends = []
        for layer in range(GMAX):
            member = members_ref[(part * groups + index) * GMAX + layer]
            holder, local = member >> 1, member & 1
            rows = held_ref[holder, local]
            for block in range(blocks):
                out_ref[part, index, KEPT * block + layer] = lanes(rows, block)
            end = held_ref[holder, 2].astype(F32)
            turned = pltpu.roll(end, TILE // 2, 0)
            ends.append(jnp.where(local == layer % 2, end, turned))
        pair = jnp.where(upper, ends[0], ends[1]).astype(BF16)
        for block in range(blocks):
            out_ref[part, index, KEPT * block + GMAX] = lanes(pair, block)
        last = pltpu.roll(ends[2], TILE // 2, 0)
        for block in range(KEPT):
            low = lanes(last, block + KEPT) if block + KEPT < blocks else 0.0
            value = jnp.where(upper_block, lanes(ends[2], block), low)
            out_ref[part, index, KEPT * blocks + block] = value.astype(BF16)

    copies = []
    for part in range(parts):

        def several(index, carry, part=part):
            for k in range(UNROLL):
                regroup(part, index * UNROLL + k)
            return carry

        lax.fori_loop(0, groups // UNROLL, several, 0)
        copies.append(
            pltpu.make_async_copy(
                out_ref.at[part], out_hbm.at[pl.ds(part * groups, groups)], sems.at[part]
            )
        )
        copies[-1].start()
    for copy in copies:
        copy.wait()


def regroup_rows(held, members):
    group_count, _, _, width = held.shape
    parts = 4
    tiles = KEPT * (width // LANES) + KEPT
    return pl.pallas_call(
        regroup_kernel,
        out_shape=pltpu.HBM((group_count, tiles, TILE, LANES), BF16),
        in_specs=[
            pl.BlockSpec(memory_space=pltpu.SMEM),
            pl.BlockSpec(memory_space=pltpu.VMEM),
        ],
        out_specs=pl.BlockSpec(memory_space=pltpu.HBM),
        scratch_shapes=[
            pltpu.VMEM((parts, group_count // parts, tiles, TILE, LANES), BF16),
            pltpu.SemaphoreType.DMA((parts,)),
        ],
        compiler_params=pltpu.CompilerParams(vmem_limit_bytes=16 * 1024 * 1024),
        cost_estimate=pl.CostEstimate(
            flops=0, bytes_accessed=7_500_000, transcendentals=0
        ),
        name="regroup_rows",
    )(members, held)


def invert_kernel(rows_ref, after_ref, maps_ref, turned_ref, sys_ref):
    del after_ref
    count, blocks = rows_ref.shape[:2]
    width = count * BLK
    kept = blocks * KEPT * TILE
    ends = blocks * TILE
    diag = lax.broadcasted_iota(jnp.int32, (BLK, BLK), 0) == lax.broadcasted_iota(
        jnp.int32, (BLK, BLK), 1
    )

    def span(index):
        return pl.ds(pl.multiple_of(index * BLK, BLK), BLK)

    def turn(i, carry):
        turned_ref[span(i), :kept] = rows_ref[i, :, :KEPT].reshape(kept, BLK).T
        last = rows_ref[i, :, KEPT].reshape(ends, BLK)
        turned_ref[span(i), kept:] = last.T
        return carry

    lax.fori_loop(0, count, turn, 0)

    def gram_block(index, carry):
        i, j = index // count, index % count
        value = dot(turned_ref[span(i), :kept], rows_ref[j, :, :KEPT].reshape(kept, BLK))
        last = rows_ref[j, :, KEPT].reshape(ends, BLK)
        sys_ref[span(i), span(j)] = value + dot(turned_ref[span(i), kept:], last)
        return carry

    lax.fori_loop(0, count * count, gram_block, 0)
    trace = jnp.float32(0)
    for i in range(count):
        here = slice(i * BLK, (i + 1) * BLK)
        trace = trace + jnp.sum(jnp.where(diag, sys_ref[here, here], 0.0))
    ridge = damping * trace / width + epsilon
    for i in range(count):
        here = slice(i * BLK, (i + 1) * BLK)
        sys_ref[here, here] = sys_ref[here, here] + jnp.where(diag, ridge, 0.0)

    def sweep(k, carry):
        inverse = block_inverse(sys_ref[span(k), span(k)], ridge)
        inverse_parts = thirds(inverse)
        panel = dot6(inverse_parts, thirds(sys_ref[span(k), :]))
        panel_parts = thirds(panel)

        def eliminate(i, inner):
            @pl.when(i != k)
            def _():
                left = thirds(sys_ref[span(i), span(k)])
                sys_ref[span(i), :] = sys_ref[span(i), :] - dot6(left, panel_parts)
                sys_ref[span(i), span(k)] = dot6(left, inverse_parts)

            return inner

        lax.fori_loop(0, count, eliminate, 0)
        sys_ref[span(k), :] = panel
        sys_ref[span(k), span(k)] = -inverse
        return carry

    lax.fori_loop(0, count, sweep, 0)

    def map_block(index, carry):
        i, j = index // strips, index % strips
        here = pl.ds(pl.multiple_of(j * strip, strip), strip)
        both = jnp.concatenate(halves(-sys_ref[span(i), :]), axis=0)
        value = dot(both, turned_ref[:, here])
        high, low = halves(value[:BLK] + value[BLK:])
        maps_ref[span(2 * i), here] = high
        maps_ref[span(2 * i + 1), here] = low
        return carry

    strip = 2 * BLK
    strips = (kept + ends) // strip
    lax.fori_loop(0, count * strips, map_block, 0)


def invert_gram(rows, after):
    count, blocks, _, _, _ = rows.shape
    width = count * BLK
    slots = blocks * TILE * OWNED
    return pl.pallas_call(
        invert_kernel,
        out_shape=jax.ShapeDtypeStruct((2 * width, slots), BF16),
        in_specs=[
            pl.BlockSpec(memory_space=pltpu.VMEM),
            pl.BlockSpec(memory_space=pl.ANY),
        ],
        out_specs=pl.BlockSpec(memory_space=pltpu.VMEM),
        scratch_shapes=[pltpu.VMEM((width, slots), BF16), pltpu.VMEM((width, width), F32)],
        compiler_params=pltpu.CompilerParams(vmem_limit_bytes=VMEM_GRANT),
        cost_estimate=pl.CostEstimate(
            flops=60_000_000_000, bytes_accessed=16_000_000, transcendentals=0
        ),
        name="invert_gram",
    )(rows, after)


def merge_kernel(
    packed_hbm, maps_hbm, out_hbm, packed_ref, maps_ref, rows_ref, out_ref, sems, out_sems
):
    groups = packed_ref.shape[0]
    size, width = out_ref.shape
    blocks = width // LANES
    kept = groups * KEPT * TILE
    ends = groups * TILE
    first = pltpu.make_async_copy(packed_hbm, packed_ref, sems.at[0])
    first.start()
    copies = []
    for index in range(size // BLK):
        here = slice(2 * index * BLK, 2 * (index + 1) * BLK)
        copies.append(
            pltpu.make_async_copy(maps_hbm.at[here], maps_ref.at[here], sems.at[index + 1])
        )
        copies[-1].start()
    first.wait()
    for block in range(blocks):
        lanes = slice(block * LANES, (block + 1) * LANES)
        rows = packed_ref[:, KEPT * block : KEPT * block + KEPT]
        rows_ref[:kept, lanes] = rows.reshape(kept, LANES)
        last = packed_ref[:, KEPT * blocks + block % KEPT].reshape(ends, LANES)
        if block >= KEPT:
            last = pltpu.roll(last.astype(F32), ends - TILE // 2, 0).astype(BF16)
        rows_ref[kept:, lanes] = last
    stores = []
    for index, copy in enumerate(copies):
        copy.wait()
        value = dot(maps_ref[2 * index * BLK : 2 * (index + 1) * BLK], rows_ref[...])
        here = slice(index * BLK, (index + 1) * BLK)
        out_ref[here] = (value[:BLK] + value[BLK:]).astype(BF16)
        stores.append(
            pltpu.make_async_copy(out_ref.at[here], out_hbm.at[here], out_sems.at[index])
        )
        stores[-1].start()
    for store in stores:
        store.wait()


def merge_rows(packed, maps):
    size, slots = maps.shape
    width = (packed.shape[1] // KEPT - 1) * LANES
    return pl.pallas_call(
        merge_kernel,
        out_shape=pltpu.HBM((size // 2, width), BF16),
        in_specs=[pl.BlockSpec(memory_space=pl.ANY)] * 2,
        out_specs=pl.BlockSpec(memory_space=pltpu.HBM),
        scratch_shapes=[
            pltpu.VMEM(packed.shape, BF16),
            pltpu.VMEM(maps.shape, BF16),
            pltpu.VMEM((slots, width), BF16),
            pltpu.VMEM((size // 2, width), BF16),
            pltpu.SemaphoreType.DMA((1 + size // (2 * BLK),)),
            pltpu.SemaphoreType.DMA((size // (2 * BLK),)),
        ],
        compiler_params=pltpu.CompilerParams(vmem_limit_bytes=VMEM_GRANT),
        cost_estimate=pl.CostEstimate(
            flops=9_400_000_000, bytes_accessed=16_000_000, transcendentals=0
        ),
        name="merge_rows",
    )(packed, maps)


def member_places(merge_group, group_count):
    experts = merge_group.shape[0]
    index = jnp.arange(experts, dtype=jnp.int32)
    earlier = index[None, :] < index[:, None]
    rank = jnp.sum(
        (merge_group[:, None] == merge_group[None, :]) & earlier, axis=1, dtype=jnp.int32
    )
    place = merge_group * GMAX + rank
    wanted = jnp.arange(group_count * GMAX, dtype=jnp.int32)
    members = jnp.sum(jnp.where(place[None, :] == wanted[:, None], index[None, :], 0), axis=1)
    chunk = merge_group * (OWNED * TILE)
    bases = [chunk + rank * TILE, chunk + GMAX * TILE + rank * (TILE // 2) - TILE]
    return members, jnp.stack(bases, axis=1)


def exchange(rows):
    return lax.all_to_all(rows, "expert", split_axis=0, concat_axis=0, tiled=True)


def on_device(routes, routed_hidden, down_proj, merge_group):
    group_count = lax.axis_size("expert")
    parts = lax.axis_size("mp")
    full_width, out_part = down_proj.shape[1:]
    tok_count, top_count, hidden_part = routed_hidden.shape
    row_count = tok_count * top_count
    experts = merge_group.shape[0]

    rows = routed_hidden.reshape(row_count, hidden_part)
    targets = routes.reshape(1, row_count)
    index = jnp.arange(experts, dtype=jnp.int32)
    chunk, local = index // 2 * (HELD * TILE), index % 2
    held_bases = jnp.stack(
        [chunk + local * TILE, chunk + 2 * TILE + local * (TILE // 2) - TILE], axis=1
    )
    members, owned_bases = member_places(merge_group, group_count)

    to_holder = pack_rows(
        targets, held_bases, rows, group_count * HELD * TILE, "pack_held"
    ).reshape(group_count, HELD * TILE, hidden_part)
    to_owner = pack_rows(
        targets, owned_bases, rows, group_count * OWNED * TILE, "pack_owned"
    ).reshape(group_count, OWNED * TILE, hidden_part)
    at_holder = exchange(to_holder)
    at_holder, to_owner = lax.optimization_barrier((at_holder, to_owner))
    held = lax.all_gather(at_holder, "mp", axis=0)
    at_owner = exchange(to_owner)

    projected = project_rows(
        held.reshape(parts, group_count, HELD, TILE, hidden_part), down_proj
    )
    home = exchange(projected.reshape(group_count, HELD * TILE, out_part))
    owned = lax.all_gather(at_owner, "mp", axis=0)
    regrouped = regroup_rows(home.reshape(group_count, HELD, TILE, out_part), members)
    arrived = exchange(regrouped)

    maps = invert_gram(
        owned.reshape(parts, group_count, OWNED, TILE, hidden_part), regrouped
    )
    merged = merge_rows(arrived, maps)
    return merged.reshape(1, full_width, out_part)


def solution(mesh):
    return jax.shard_map(
        on_device,
        mesh=mesh,
        in_specs=(P("expert", None), P("expert", None, "mp"), P("expert", None, "mp"), P()),
        out_specs=P("expert", None, "mp"),
        check_vma=False,
    )
```

```python
import jax
import jax.numpy as jnp
from jax import lax
from jax.experimental import pallas as pl
from jax.experimental.pallas import tpu as pltpu
from jax.sharding import PartitionSpec as P

GMAX = 3
BLK = 256
damping = 0.1
epsilon = 1e-05
F32 = jnp.float32
BF16 = jnp.bfloat16


def sweep_counts():
    gaps, delta = [], 1e-3
    for _ in range(16):
        gaps.append(1.0 - delta)
        if 2.0 * delta / (1.0 + delta) > 2.0 - 2.0 / GAIN_MAX:
            delta = (1.0 - (1.0 - delta) / GAIN_MAX) ** 0.5
        else:
            delta = (2.0 * delta / (1.0 + delta)) ** 0.5
    return gaps


GAIN_MAX = 1.85
NEWTON_GAPS = sweep_counts()


def halves(value):
    high = value.astype(BF16)
    return high, (value - high.astype(F32)).astype(BF16)


def dot(a, b):
    return jnp.dot(a, b, preferred_element_type=F32)


def dot3(a, b):
    (ah, al), (bh, bl) = a, b
    return dot(ah, bh) + (dot(ah, bl) + dot(al, bh))


def thirds(value):
    high = value.astype(BF16)
    rest = value - high.astype(F32)
    mid = rest.astype(BF16)
    return high, mid, (rest - mid.astype(F32)).astype(BF16)


def dot6(a, b):
    (ah, am, al), (bh, bm, bl) = a, b
    small = dot(am, bm) + (dot(ah, bl) + dot(al, bh))
    return dot(ah, bh) + (dot(ah, bm) + dot(am, bh) + small)


def block_inverse(block, lower):
    size = block.shape[0]
    upper = jnp.max(jnp.sum(jnp.abs(block), axis=1, keepdims=True))
    gap = 2.0 * lower / (lower + upper)
    steps = jnp.int32(0)
    for edge in NEWTON_GAPS:
        steps = steps + (gap < edge).astype(jnp.int32)
    rows = lax.broadcasted_iota(jnp.int32, (size, size), 0)
    cols = lax.broadcasted_iota(jnp.int32, (size, size), 1)
    total = jnp.full((1, size), lower + upper, F32)
    start = jnp.where(rows == cols, 2.0 / total, 0.0)
    block_parts = thirds(block)

    def step(_, carry):
        guess, delta = carry
        parts = halves(guess)
        image = dot3(block_parts[:2], parts)
        gain = jnp.minimum(2.0 / (2.0 - delta * delta), GAIN_MAX)
        guess = gain * (2.0 * guess - dot3(parts, halves(image)))
        return guess, 1.0 - gain * (1.0 - delta * delta)

    guess, _ = lax.fori_loop(0, steps, step, (start, 1.0 - 2.0 * lower / total))
    parts = thirds(guess)
    return 2.0 * guess - dot6(parts, thirds(dot6(block_parts, parts)))


TILE = 8
HELD = 3
OWNED = 5
KEPT = 4
LANES = 128
UNROLL = 4
PROJECT_PARTS = 2
VMEM_GRANT = 58 * 1024 * 1024
WIDE_GRANT = 60 * 1024 * 1024
SMALL_GRANT = 32 * 1024 * 1024


def slot_kernel(routes_ref, bases_ref, rows_ref, out_ref, slot_ref):
    experts = bases_ref.shape[0]
    count = routes_ref.shape[1]
    hit = lax.broadcasted_iota(jnp.int32, (experts, count), 0) == routes_ref[...]
    onehot = jnp.where(hit, 1.0, 0.0).astype(BF16)
    order = lax.broadcasted_iota(jnp.int32, (count, count), 0) < lax.broadcasted_iota(
        jnp.int32, (count, count), 1
    )
    before = dot(onehot, jnp.where(order, 1.0, 0.0).astype(BF16))
    bases = bases_ref[...].astype(F32)
    place = before + jnp.where(before < TILE, bases[:, 0:1], bases[:, 1:2])
    slot = jnp.sum(jnp.where(hit, place, 0.0), axis=0, keepdims=True)
    slot_ref[...] = slot.astype(jnp.int32)

    def fill(index, carry):
        here = pl.multiple_of(index * BLK, BLK)
        wanted = lax.broadcasted_iota(jnp.int32, (BLK, count), 0) + here
        pick = jnp.where(wanted == slot_ref[...], 1.0, 0.0).astype(BF16)
        out_ref[pl.ds(here, BLK), :] = dot(pick, rows_ref[...]).astype(BF16)
        return carry

    lax.fori_loop(0, out_ref.shape[0] // BLK, fill, 0)


def pack_rows(routes, bases, rows, slots, grant, name):
    count, width = rows.shape
    return pl.pallas_call(
        slot_kernel,
        out_shape=jax.ShapeDtypeStruct((slots, width), BF16),
        in_specs=[pl.BlockSpec(memory_space=pltpu.VMEM)] * 3,
        out_specs=pl.BlockSpec(memory_space=pltpu.VMEM),
        scratch_shapes=[pltpu.VMEM((1, count), jnp.int32)],
        compiler_params=pltpu.CompilerParams(vmem_limit_bytes=grant),
        cost_estimate=pl.CostEstimate(
            flops=3_000_000_000, bytes_accessed=2_000_000, transcendentals=0
        ),
        name=name,
    )(routes, bases, rows)


def project_kernel(
    rows_hbm, weights_hbm, out_hbm, rows_ref, weights_ref, out_ref, mixed_ref, row_sems, weight_sems, out_sems
):
    parts, blocks = rows_ref.shape[:2]
    width = out_ref.shape[3]
    locals_count = weights_ref.shape[0]
    step = blocks // PROJECT_PARTS
    slots = step * TILE
    upper = lax.broadcasted_iota(jnp.int32, (slots, 1), 0) % TILE < TILE // 2

    def load_rows(part):
        here = pl.ds(part * step, step)
        return pltpu.make_async_copy(
            rows_hbm.at[:, here], rows_ref.at[:, here], row_sems.at[part]
        )

    def load_weights(local):
        return pltpu.make_async_copy(
            weights_hbm.at[local], weights_ref.at[local], weight_sems.at[local]
        )

    loads = [load_rows(0), load_weights(0)]
    loads += [load_rows(part) for part in range(1, PROJECT_PARTS)]
    loads += [load_weights(local) for local in range(1, locals_count)]
    for load in loads:
        load.start()
    stores = []

    def store(part, tile):
        here = pl.ds(part * step, step)
        copy = pltpu.make_async_copy(
            out_ref.at[here, tile], out_hbm.at[here, tile], out_sems.at[part, tile]
        )
        copy.start()
        stores.append(copy)

    for local in range(locals_count):
        for part in range(PROJECT_PARTS):
            here = slice(part * step, (part + 1) * step)
            if local == 0:
                load_rows(part).wait()
            if part == 0:
                load_weights(local).wait()

            def tile_rows(tile, here=here):
                return jnp.concatenate(
                    [rows_ref[m, here, tile].reshape(slots, -1) for m in range(parts)], axis=1
                )

            ends = tile_rows(2)
            none = jnp.zeros_like(ends)
            end = jnp.where(upper, ends, none) if local == 0 else jnp.where(upper, none, ends)
            rows = jnp.concatenate([tile_rows(local), end], axis=0)
            value = dot(rows, weights_ref[local])
            out_ref[here, local] = value[:slots].astype(BF16).reshape(step, TILE, width)
            store(part, local)
            if local == 0:
                mixed_ref[part] = value[slots:]
            else:
                mixed = mixed_ref[part] + value[slots:]
                out_ref[here, 2] = mixed.astype(BF16).reshape(step, TILE, width)
                store(part, 2)
    for copy in stores:
        copy.wait()


def project_rows(rows, weights):
    parts, blocks, _, _, hidden_part = rows.shape
    width = weights.shape[2]
    shape = (blocks, HELD, TILE, width)
    return pl.pallas_call(
        project_kernel,
        out_shape=pltpu.HBM(shape, BF16),
        in_specs=[pl.BlockSpec(memory_space=pl.ANY)] * 2,
        out_specs=pl.BlockSpec(memory_space=pltpu.HBM),
        scratch_shapes=[
            pltpu.VMEM(rows.shape, BF16),
            pltpu.VMEM(weights.shape, BF16),
            pltpu.VMEM(shape, BF16),
            pltpu.VMEM((PROJECT_PARTS, blocks // PROJECT_PARTS * TILE, width), F32),
            pltpu.SemaphoreType.DMA((PROJECT_PARTS,)),
            pltpu.SemaphoreType.DMA((weights.shape[0],)),
            pltpu.SemaphoreType.DMA((PROJECT_PARTS, HELD)),
        ],
        compiler_params=pltpu.CompilerParams(vmem_limit_bytes=WIDE_GRANT),
        cost_estimate=pl.CostEstimate(
            flops=4_000_000_000, bytes_accessed=10_000_000, transcendentals=0
        ),
        name="project_rows",
    )(rows, weights)


def regroup_kernel(members_ref, held_ref, out_hbm, out_ref, sems):
    parts, groups = out_ref.shape[:2]
    width = held_ref.shape[3]
    blocks = width // LANES
    upper = lax.broadcasted_iota(jnp.int32, (TILE, width), 0) < TILE // 2
    upper_block = upper[:, :LANES]

    def lanes(value, block):
        return value[:, block * LANES : (block + 1) * LANES]

    def regroup(part, index):
        ends = []
        for layer in range(GMAX):
            member = members_ref[(part * groups + index) * GMAX + layer]
            holder, local = member >> 1, member & 1
            rows = held_ref[holder, local]
            for block in range(blocks):
                out_ref[part, index, KEPT * block + layer] = lanes(rows, block)
            end = held_ref[holder, 2].astype(F32)
            turned = pltpu.roll(end, TILE // 2, 0)
            ends.append(jnp.where(local == layer % 2, end, turned))
        pair = jnp.where(upper, ends[0], ends[1]).astype(BF16)
        for block in range(blocks):
            out_ref[part, index, KEPT * block + GMAX] = lanes(pair, block)
        last = pltpu.roll(ends[2], TILE // 2, 0)
        for block in range(KEPT):
            low = lanes(last, block + KEPT) if block + KEPT < blocks else 0.0
            value = jnp.where(upper_block, lanes(ends[2], block), low)
            out_ref[part, index, KEPT * blocks + block] = value.astype(BF16)

    copies = []
    for part in range(parts):

        def several(index, carry, part=part):
            for k in range(UNROLL):
                regroup(part, index * UNROLL + k)
            return carry

        lax.fori_loop(0, groups // UNROLL, several, 0)
        copies.append(
            pltpu.make_async_copy(
                out_ref.at[part], out_hbm.at[pl.ds(part * groups, groups)], sems.at[part]
            )
        )
        copies[-1].start()
    for copy in copies:
        copy.wait()


def regroup_rows(held, members):
    group_count, _, _, width = held.shape
    parts = 4
    tiles = KEPT * (width // LANES) + KEPT
    return pl.pallas_call(
        regroup_kernel,
        out_shape=pltpu.HBM((group_count, tiles, TILE, LANES), BF16),
        in_specs=[
            pl.BlockSpec(memory_space=pltpu.SMEM),
            pl.BlockSpec(memory_space=pltpu.VMEM),
        ],
        out_specs=pl.BlockSpec(memory_space=pltpu.HBM),
        scratch_shapes=[
            pltpu.VMEM((parts, group_count // parts, tiles, TILE, LANES), BF16),
            pltpu.SemaphoreType.DMA((parts,)),
        ],
        compiler_params=pltpu.CompilerParams(vmem_limit_bytes=16 * 1024 * 1024),
        cost_estimate=pl.CostEstimate(
            flops=0, bytes_accessed=7_500_000, transcendentals=0
        ),
        name="regroup_rows",
    )(members, held)


def pair_ends(first, second, lower):
    shape = first.shape
    first, second = (part.astype(F32).reshape(-1, shape[-1]) for part in (first, second))
    upper = lax.broadcasted_iota(jnp.int32, first.shape, 0) % TILE < TILE // 2
    if lower:
        first = pltpu.roll(first, first.shape[0] - TILE // 2, 0)
    else:
        second = pltpu.roll(second, TILE // 2, 0)
    return jnp.where(upper, first, second).astype(BF16)


def invert_kernel(rows_ref, after_ref, maps_ref, turned_ref, sys_ref):
    del after_ref
    count, blocks = rows_ref.shape[:2]
    width = count * BLK
    kept = blocks * KEPT * TILE
    ends = blocks * TILE // 2
    diag = lax.broadcasted_iota(jnp.int32, (BLK, BLK), 0) == lax.broadcasted_iota(
        jnp.int32, (BLK, BLK), 1
    )

    def span(index):
        return pl.ds(pl.multiple_of(index * BLK, BLK), BLK)

    def end_rows(i):
        last = rows_ref[i, :, KEPT].reshape(blocks // 2, 2, TILE, BLK)
        return pair_ends(last[:, 0], last[:, 1], False)

    def turn(i, carry):
        turned_ref[span(i), :kept] = rows_ref[i, :, :KEPT].reshape(kept, BLK).T
        turned_ref[span(i), kept:] = end_rows(i).T
        return carry

    lax.fori_loop(0, count, turn, 0)

    def gram_block(index, carry):
        i, j = index // count, index % count
        value = dot(turned_ref[span(i), :kept], rows_ref[j, :, :KEPT].reshape(kept, BLK))
        sys_ref[span(i), span(j)] = value + dot(turned_ref[span(i), kept:], end_rows(j))
        return carry

    lax.fori_loop(0, count * count, gram_block, 0)
    trace = jnp.float32(0)
    for i in range(count):
        here = slice(i * BLK, (i + 1) * BLK)
        trace = trace + jnp.sum(jnp.where(diag, sys_ref[here, here], 0.0))
    ridge = damping * trace / width + epsilon
    for i in range(count):
        here = slice(i * BLK, (i + 1) * BLK)
        sys_ref[here, here] = sys_ref[here, here] + jnp.where(diag, ridge, 0.0)

    def sweep(k, carry):
        inverse = block_inverse(sys_ref[span(k), span(k)], ridge)
        inverse_parts = thirds(inverse)
        panel = dot6(inverse_parts, thirds(sys_ref[span(k), :]))
        panel_parts = thirds(panel)

        def eliminate(i, inner):
            @pl.when(i != k)
            def _():
                left = thirds(sys_ref[span(i), span(k)])
                sys_ref[span(i), :] = sys_ref[span(i), :] - dot6(left, panel_parts)
                sys_ref[span(i), span(k)] = dot6(left, inverse_parts)

            return inner

        lax.fori_loop(0, count, eliminate, 0)
        sys_ref[span(k), :] = panel
        sys_ref[span(k), span(k)] = -inverse
        return carry

    lax.fori_loop(0, count, sweep, 0)

    def map_block(index, carry):
        i, j = index // strips, index % strips
        here = pl.ds(pl.multiple_of(j * strip, strip), strip)
        both = jnp.concatenate(halves(-sys_ref[span(i), :]), axis=0)
        value = dot(both, turned_ref[:, here])
        high, low = halves(value[:BLK] + value[BLK:])
        maps_ref[span(2 * i), here] = high
        maps_ref[span(2 * i + 1), here] = low
        return carry

    strip = 3 * BLK
    strips = (kept + ends) // strip
    lax.fori_loop(0, count * strips, map_block, 0)


def invert_gram(rows, after):
    count, blocks, _, _, _ = rows.shape
    width = count * BLK
    slots = blocks * TILE * KEPT + blocks * TILE // 2
    return pl.pallas_call(
        invert_kernel,
        out_shape=jax.ShapeDtypeStruct((2 * width, slots), BF16),
        in_specs=[
            pl.BlockSpec(memory_space=pltpu.VMEM),
            pl.BlockSpec(memory_space=pl.ANY),
        ],
        out_specs=pl.BlockSpec(memory_space=pltpu.VMEM),
        scratch_shapes=[pltpu.VMEM((width, slots), BF16), pltpu.VMEM((width, width), F32)],
        compiler_params=pltpu.CompilerParams(vmem_limit_bytes=VMEM_GRANT),
        cost_estimate=pl.CostEstimate(
            flops=60_000_000_000, bytes_accessed=16_000_000, transcendentals=0
        ),
        name="invert_gram",
    )(rows, after)


def merge_kernel(
    packed_hbm, maps_hbm, out_hbm, packed_ref, maps_ref, rows_ref, out_ref, sems, out_sems
):
    groups = packed_ref.shape[0]
    size, width = out_ref.shape
    blocks = width // LANES
    kept = groups * KEPT * TILE
    first = pltpu.make_async_copy(packed_hbm, packed_ref, sems.at[0])
    first.start()
    copies = []
    for index in range(size // BLK):
        here = slice(2 * index * BLK, 2 * (index + 1) * BLK)
        copies.append(
            pltpu.make_async_copy(maps_hbm.at[here], maps_ref.at[here], sems.at[index + 1])
        )
        copies[-1].start()
    first.wait()
    for block in range(blocks):
        lanes = slice(block * LANES, (block + 1) * LANES)
        rows = packed_ref[:, KEPT * block : KEPT * block + KEPT]
        rows_ref[:kept, lanes] = rows.reshape(kept, LANES)
        last = packed_ref[:, KEPT * blocks + block % KEPT]
        last = last.reshape(groups // 2, 2, TILE, LANES)
        rows_ref[kept:, lanes] = pair_ends(last[:, 0], last[:, 1], block >= KEPT)
    stores = []
    for index, copy in enumerate(copies):
        copy.wait()
        value = dot(maps_ref[2 * index * BLK : 2 * (index + 1) * BLK], rows_ref[...])
        here = slice(index * BLK, (index + 1) * BLK)
        out_ref[here] = (value[:BLK] + value[BLK:]).astype(BF16)
        stores.append(
            pltpu.make_async_copy(out_ref.at[here], out_hbm.at[here], out_sems.at[index])
        )
        stores[-1].start()
    for store in stores:
        store.wait()


def merge_rows(packed, maps):
    size, slots = maps.shape
    width = (packed.shape[1] // KEPT - 1) * LANES
    return pl.pallas_call(
        merge_kernel,
        out_shape=pltpu.HBM((size // 2, width), BF16),
        in_specs=[pl.BlockSpec(memory_space=pl.ANY)] * 2,
        out_specs=pl.BlockSpec(memory_space=pltpu.HBM),
        scratch_shapes=[
            pltpu.VMEM(packed.shape, BF16),
            pltpu.VMEM(maps.shape, BF16),
            pltpu.VMEM((slots, width), BF16),
            pltpu.VMEM((size // 2, width), BF16),
            pltpu.SemaphoreType.DMA((1 + size // (2 * BLK),)),
            pltpu.SemaphoreType.DMA((size // (2 * BLK),)),
        ],
        compiler_params=pltpu.CompilerParams(vmem_limit_bytes=VMEM_GRANT),
        cost_estimate=pl.CostEstimate(
            flops=9_400_000_000, bytes_accessed=16_000_000, transcendentals=0
        ),
        name="merge_rows",
    )(packed, maps)


def member_places(merge_group, group_count):
    experts = merge_group.shape[0]
    index = jnp.arange(experts, dtype=jnp.int32)
    earlier = index[None, :] < index[:, None]
    rank = jnp.sum(
        (merge_group[:, None] == merge_group[None, :]) & earlier, axis=1, dtype=jnp.int32
    )
    place = merge_group * GMAX + rank
    wanted = jnp.arange(group_count * GMAX, dtype=jnp.int32)
    members = jnp.sum(jnp.where(place[None, :] == wanted[:, None], index[None, :], 0), axis=1)
    chunk = merge_group * (OWNED * TILE)
    bases = [chunk + rank * TILE, chunk + GMAX * TILE + rank * (TILE // 2) - TILE]
    return members, jnp.stack(bases, axis=1)


def exchange(rows):
    return lax.all_to_all(rows, "expert", split_axis=0, concat_axis=0, tiled=True)


def on_device(routes, routed_hidden, down_proj, merge_group):
    group_count = lax.axis_size("expert")
    parts = lax.axis_size("mp")
    full_width, out_part = down_proj.shape[1:]
    tok_count, top_count, hidden_part = routed_hidden.shape
    row_count = tok_count * top_count
    experts = merge_group.shape[0]

    rows = routed_hidden.reshape(row_count, hidden_part)
    targets = routes.reshape(1, row_count)
    index = jnp.arange(experts, dtype=jnp.int32)
    chunk, local = index // 2 * (HELD * TILE), index % 2
    held_bases = jnp.stack(
        [chunk + local * TILE, chunk + 2 * TILE + local * (TILE // 2) - TILE], axis=1
    )
    members, owned_bases = member_places(merge_group, group_count)

    to_holder = pack_rows(
        targets, held_bases, rows, group_count * HELD * TILE, SMALL_GRANT, "pack_held"
    ).reshape(group_count, HELD * TILE, hidden_part)
    to_owner = pack_rows(
        targets, owned_bases, rows, group_count * OWNED * TILE, WIDE_GRANT, "pack_owned"
    ).reshape(group_count, OWNED * TILE, hidden_part)
    at_holder = exchange(to_holder)
    at_holder, to_owner = lax.optimization_barrier((at_holder, to_owner))
    held = lax.all_gather(at_holder, "mp", axis=0)
    at_owner = exchange(to_owner)

    projected = project_rows(
        held.reshape(parts, group_count, HELD, TILE, hidden_part), down_proj
    )
    home = exchange(projected.reshape(group_count, HELD * TILE, out_part))
    owned = lax.all_gather(at_owner, "mp", axis=0)
    regrouped = regroup_rows(home.reshape(group_count, HELD, TILE, out_part), members)
    arrived = exchange(regrouped)

    maps = invert_gram(
        owned.reshape(parts, group_count, OWNED, TILE, hidden_part), regrouped
    )
    merged = merge_rows(arrived, maps)
    return merged.reshape(1, full_width, out_part)


def solution(mesh):
    return jax.shard_map(
        on_device,
        mesh=mesh,
        in_specs=(P("expert", None), P("expert", None, "mp"), P("expert", None, "mp"), P()),
        out_specs=P("expert", None, "mp"),
        check_vma=False,
    )
```

```python
import jax
import jax.numpy as jnp
from jax import lax
from jax.experimental import pallas as pl
from jax.experimental.pallas import tpu as pltpu
from jax.sharding import PartitionSpec as P

GMAX = 3
BLK = 256
damping = 0.1
epsilon = 1e-05
F32 = jnp.float32
BF16 = jnp.bfloat16


def sweep_counts():
    gaps, delta = [], 1e-3
    for _ in range(16):
        gaps.append(1.0 - delta)
        if 2.0 * delta / (1.0 + delta) > 2.0 - 2.0 / GAIN_MAX:
            delta = (1.0 - (1.0 - delta) / GAIN_MAX) ** 0.5
        else:
            delta = (2.0 * delta / (1.0 + delta)) ** 0.5
    return gaps


GAIN_MAX = 1.85
NEWTON_GAPS = sweep_counts()


def halves(value):
    high = value.astype(BF16)
    return high, (value - high.astype(F32)).astype(BF16)


def dot(a, b):
    return jnp.dot(a, b, preferred_element_type=F32)


def dot3(a, b):
    (ah, al), (bh, bl) = a, b
    return dot(ah, bh) + (dot(ah, bl) + dot(al, bh))


def thirds(value):
    high = value.astype(BF16)
    rest = value - high.astype(F32)
    mid = rest.astype(BF16)
    return high, mid, (rest - mid.astype(F32)).astype(BF16)


def dot6(a, b):
    (ah, am, al), (bh, bm, bl) = a, b
    small = dot(am, bm) + (dot(ah, bl) + dot(al, bh))
    return dot(ah, bh) + (dot(ah, bm) + dot(am, bh) + small)


def block_inverse(block, lower):
    size = block.shape[0]
    upper = jnp.max(jnp.sum(jnp.abs(block), axis=1, keepdims=True))
    gap = 2.0 * lower / (lower + upper)
    steps = jnp.int32(0)
    for edge in NEWTON_GAPS:
        steps = steps + (gap < edge).astype(jnp.int32)
    rows = lax.broadcasted_iota(jnp.int32, (size, size), 0)
    cols = lax.broadcasted_iota(jnp.int32, (size, size), 1)
    total = jnp.full((1, size), lower + upper, F32)
    start = jnp.where(rows == cols, 2.0 / total, 0.0)
    block_parts = thirds(block)

    def step(_, carry):
        guess, delta = carry
        parts = halves(guess)
        image = dot3(block_parts[:2], parts)
        gain = jnp.minimum(2.0 / (2.0 - delta * delta), GAIN_MAX)
        guess = gain * (2.0 * guess - dot3(parts, halves(image)))
        return guess, 1.0 - gain * (1.0 - delta * delta)

    guess, _ = lax.fori_loop(0, steps, step, (start, 1.0 - 2.0 * lower / total))
    parts = thirds(guess)
    return 2.0 * guess - dot6(parts, thirds(dot6(block_parts, parts)))


TILE = 8
HELD = 3
OWNED = 5
KEPT = 4
LANES = 128
UNROLL = 4
PROJECT_PARTS = 2
VMEM_GRANT = 58 * 1024 * 1024
WIDE_GRANT = 60 * 1024 * 1024
SMALL_GRANT = 32 * 1024 * 1024


def slot_kernel(routes_ref, bases_ref, rows_ref, out_ref, slot_ref):
    experts = bases_ref.shape[0]
    count = routes_ref.shape[1]
    hit = lax.broadcasted_iota(jnp.int32, (experts, count), 0) == routes_ref[...]
    onehot = jnp.where(hit, 1.0, 0.0).astype(BF16)
    order = lax.broadcasted_iota(jnp.int32, (count, count), 0) < lax.broadcasted_iota(
        jnp.int32, (count, count), 1
    )
    before = dot(onehot, jnp.where(order, 1.0, 0.0).astype(BF16))
    bases = bases_ref[...].astype(F32)
    place = before + jnp.where(before < TILE, bases[:, 0:1], bases[:, 1:2])
    slot = jnp.sum(jnp.where(hit, place, 0.0), axis=0, keepdims=True)
    slot_ref[...] = slot.astype(jnp.int32)

    def fill(index, carry):
        here = pl.multiple_of(index * BLK, BLK)
        wanted = lax.broadcasted_iota(jnp.int32, (BLK, count), 0) + here
        pick = jnp.where(wanted == slot_ref[...], 1.0, 0.0).astype(BF16)
        out_ref[pl.ds(here, BLK), :] = dot(pick, rows_ref[...]).astype(BF16)
        return carry

    lax.fori_loop(0, out_ref.shape[0] // BLK, fill, 0)


def pack_rows(routes, bases, rows, slots, grant, name):
    count, width = rows.shape
    return pl.pallas_call(
        slot_kernel,
        out_shape=jax.ShapeDtypeStruct((slots, width), BF16),
        in_specs=[pl.BlockSpec(memory_space=pltpu.VMEM)] * 3,
        out_specs=pl.BlockSpec(memory_space=pltpu.VMEM),
        scratch_shapes=[pltpu.VMEM((1, count), jnp.int32)],
        compiler_params=pltpu.CompilerParams(vmem_limit_bytes=grant),
        cost_estimate=pl.CostEstimate(
            flops=3_000_000_000, bytes_accessed=2_000_000, transcendentals=0
        ),
        name=name,
    )(routes, bases, rows)


def project_kernel(
    rows_hbm, weights_hbm, out_hbm, rows_ref, weights_ref, out_ref, mixed_ref, row_sems, weight_sems, out_sems
):
    parts, blocks = rows_ref.shape[:2]
    width = out_ref.shape[3]
    locals_count = weights_ref.shape[0]
    step = blocks // PROJECT_PARTS
    slots = step * TILE
    upper = lax.broadcasted_iota(jnp.int32, (slots, 1), 0) % TILE < TILE // 2

    def load_rows(part):
        here = pl.ds(part * step, step)
        return pltpu.make_async_copy(
            rows_hbm.at[:, here], rows_ref.at[:, here], row_sems.at[part]
        )

    def load_weights(local):
        return pltpu.make_async_copy(
            weights_hbm.at[local], weights_ref.at[local], weight_sems.at[local]
        )

    loads = [load_rows(0), load_weights(0)]
    loads += [load_rows(part) for part in range(1, PROJECT_PARTS)]
    loads += [load_weights(local) for local in range(1, locals_count)]
    for load in loads:
        load.start()
    stores = []

    def store(part, tile):
        here = pl.ds(part * step, step)
        copy = pltpu.make_async_copy(
            out_ref.at[here, tile], out_hbm.at[here, tile], out_sems.at[part, tile]
        )
        copy.start()
        stores.append(copy)

    for local in range(locals_count):
        for part in range(PROJECT_PARTS):
            here = slice(part * step, (part + 1) * step)
            if local == 0:
                load_rows(part).wait()
            if part == 0:
                load_weights(local).wait()

            def tile_rows(tile, here=here):
                return jnp.concatenate(
                    [rows_ref[m, here, tile].reshape(slots, -1) for m in range(parts)], axis=1
                )

            ends = tile_rows(2)
            none = jnp.zeros_like(ends)
            end = jnp.where(upper, ends, none) if local == 0 else jnp.where(upper, none, ends)
            rows = jnp.concatenate([tile_rows(local), end], axis=0)
            value = dot(rows, weights_ref[local])
            out_ref[here, local] = value[:slots].astype(BF16).reshape(step, TILE, width)
            store(part, local)
            if local == 0:
                mixed_ref[part] = value[slots:]
            else:
                mixed = mixed_ref[part] + value[slots:]
                out_ref[here, 2] = mixed.astype(BF16).reshape(step, TILE, width)
                store(part, 2)
    for copy in stores:
        copy.wait()


def project_rows(rows, weights):
    parts, blocks, _, _, hidden_part = rows.shape
    width = weights.shape[2]
    shape = (blocks, HELD, TILE, width)
    return pl.pallas_call(
        project_kernel,
        out_shape=pltpu.HBM(shape, BF16),
        in_specs=[pl.BlockSpec(memory_space=pl.ANY)] * 2,
        out_specs=pl.BlockSpec(memory_space=pltpu.HBM),
        scratch_shapes=[
            pltpu.VMEM(rows.shape, BF16),
            pltpu.VMEM(weights.shape, BF16),
            pltpu.VMEM(shape, BF16),
            pltpu.VMEM((PROJECT_PARTS, blocks // PROJECT_PARTS * TILE, width), F32),
            pltpu.SemaphoreType.DMA((PROJECT_PARTS,)),
            pltpu.SemaphoreType.DMA((weights.shape[0],)),
            pltpu.SemaphoreType.DMA((PROJECT_PARTS, HELD)),
        ],
        compiler_params=pltpu.CompilerParams(vmem_limit_bytes=WIDE_GRANT),
        cost_estimate=pl.CostEstimate(
            flops=4_000_000_000, bytes_accessed=10_000_000, transcendentals=0
        ),
        name="project_rows",
    )(rows, weights)


def regroup_kernel(members_ref, held_ref, out_hbm, out_ref, sems):
    parts, groups = out_ref.shape[:2]
    width = held_ref.shape[3]
    blocks = width // LANES
    upper = lax.broadcasted_iota(jnp.int32, (TILE, width), 0) < TILE // 2
    upper_block = upper[:, :LANES]

    def lanes(value, block):
        return value[:, block * LANES : (block + 1) * LANES]

    def regroup(part, index):
        ends = []
        for layer in range(GMAX):
            member = members_ref[(part * groups + index) * GMAX + layer]
            holder, local = member >> 1, member & 1
            rows = held_ref[holder, local]
            for block in range(blocks):
                out_ref[part, index, KEPT * block + layer] = lanes(rows, block)
            end = held_ref[holder, 2].astype(F32)
            turned = pltpu.roll(end, TILE // 2, 0)
            ends.append(jnp.where(local == layer % 2, end, turned))
        pair = jnp.where(upper, ends[0], ends[1]).astype(BF16)
        for block in range(blocks):
            out_ref[part, index, KEPT * block + GMAX] = lanes(pair, block)
        last = pltpu.roll(ends[2], TILE // 2, 0)
        for block in range(KEPT):
            low = lanes(last, block + KEPT) if block + KEPT < blocks else 0.0
            value = jnp.where(upper_block, lanes(ends[2], block), low)
            out_ref[part, index, KEPT * blocks + block] = value.astype(BF16)

    copies = []
    for part in range(parts):

        def several(index, carry, part=part):
            for k in range(UNROLL):
                regroup(part, index * UNROLL + k)
            return carry

        lax.fori_loop(0, groups // UNROLL, several, 0)
        copies.append(
            pltpu.make_async_copy(
                out_ref.at[part], out_hbm.at[pl.ds(part * groups, groups)], sems.at[part]
            )
        )
        copies[-1].start()
    for copy in copies:
        copy.wait()


def regroup_rows(held, members):
    group_count, _, _, width = held.shape
    parts = 4
    tiles = KEPT * (width // LANES) + KEPT
    return pl.pallas_call(
        regroup_kernel,
        out_shape=pltpu.HBM((group_count, tiles, TILE, LANES), BF16),
        in_specs=[
            pl.BlockSpec(memory_space=pltpu.SMEM),
            pl.BlockSpec(memory_space=pltpu.VMEM),
        ],
        out_specs=pl.BlockSpec(memory_space=pltpu.HBM),
        scratch_shapes=[
            pltpu.VMEM((parts, group_count // parts, tiles, TILE, LANES), BF16),
            pltpu.SemaphoreType.DMA((parts,)),
        ],
        compiler_params=pltpu.CompilerParams(vmem_limit_bytes=16 * 1024 * 1024),
        cost_estimate=pl.CostEstimate(
            flops=0, bytes_accessed=7_500_000, transcendentals=0
        ),
        name="regroup_rows",
    )(members, held)


def pair_ends(first, second, lower):
    shape = first.shape
    first, second = (part.astype(F32).reshape(-1, shape[-1]) for part in (first, second))
    upper = lax.broadcasted_iota(jnp.int32, first.shape, 0) % TILE < TILE // 2
    if lower:
        first = pltpu.roll(first, first.shape[0] - TILE // 2, 0)
    else:
        second = pltpu.roll(second, TILE // 2, 0)
    return jnp.where(upper, first, second).astype(BF16)


def invert_kernel(rows_ref, after_ref, maps_ref, turned_ref, sys_ref):
    del after_ref
    count, blocks = rows_ref.shape[:2]
    width = count * BLK
    kept = blocks * KEPT * TILE
    ends = blocks * TILE // 2
    diag = lax.broadcasted_iota(jnp.int32, (BLK, BLK), 0) == lax.broadcasted_iota(
        jnp.int32, (BLK, BLK), 1
    )

    def span(index):
        return pl.ds(pl.multiple_of(index * BLK, BLK), BLK)

    def end_rows(i):
        last = rows_ref[i, :, KEPT].reshape(blocks // 2, 2, TILE, BLK)
        return pair_ends(last[:, 0], last[:, 1], False)

    def turn(i, carry):
        turned_ref[span(i), :kept] = rows_ref[i, :, :KEPT].reshape(kept, BLK).T
        turned_ref[span(i), kept:] = end_rows(i).T
        return carry

    lax.fori_loop(0, count, turn, 0)

    def gram_block(index, carry):
        i, j = index // count, index % count
        value = dot(turned_ref[span(i), :kept], rows_ref[j, :, :KEPT].reshape(kept, BLK))
        sys_ref[span(i), span(j)] = value + dot(turned_ref[span(i), kept:], end_rows(j))
        return carry

    lax.fori_loop(0, count * count, gram_block, 0)
    trace = jnp.float32(0)
    for i in range(count):
        here = slice(i * BLK, (i + 1) * BLK)
        trace = trace + jnp.sum(jnp.where(diag, sys_ref[here, here], 0.0))
    ridge = damping * trace / width + epsilon
    for i in range(count):
        here = slice(i * BLK, (i + 1) * BLK)
        sys_ref[here, here] = sys_ref[here, here] + jnp.where(diag, ridge, 0.0)

    def sweep(k, carry):
        inverse = block_inverse(sys_ref[span(k), span(k)], ridge)
        inverse_parts = thirds(inverse)
        panel = dot6(inverse_parts, thirds(sys_ref[span(k), :]))
        panel_parts = thirds(panel)

        def eliminate(i, inner):
            @pl.when(i != k)
            def _():
                left = thirds(sys_ref[span(i), span(k)])
                sys_ref[span(i), :] = sys_ref[span(i), :] - dot6(left, panel_parts)
                sys_ref[span(i), span(k)] = dot6(left, inverse_parts)

            return inner

        lax.fori_loop(0, count, eliminate, 0)
        sys_ref[span(k), :] = panel
        sys_ref[span(k), span(k)] = -inverse
        return carry

    lax.fori_loop(0, count, sweep, 0)

    def map_block(index, carry):
        i, j = index // strips, index % strips
        here = pl.ds(pl.multiple_of(j * strip, strip), strip)
        both = jnp.concatenate(halves(-sys_ref[span(i), :]), axis=0)
        value = dot(both, turned_ref[:, here])
        high, low = halves(value[:BLK] + value[BLK:])
        maps_ref[span(2 * i), here] = high
        maps_ref[span(2 * i + 1), here] = low
        return carry

    strip = 3 * BLK
    strips = (kept + ends) // strip
    lax.fori_loop(0, count * strips, map_block, 0)


def invert_gram(rows, after):
    count, blocks, _, _, _ = rows.shape
    width = count * BLK
    slots = blocks * TILE * KEPT + blocks * TILE // 2
    return pl.pallas_call(
        invert_kernel,
        out_shape=jax.ShapeDtypeStruct((2 * width, slots), BF16),
        in_specs=[
            pl.BlockSpec(memory_space=pltpu.VMEM),
            pl.BlockSpec(memory_space=pl.ANY),
        ],
        out_specs=pl.BlockSpec(memory_space=pltpu.VMEM),
        scratch_shapes=[pltpu.VMEM((width, slots), BF16), pltpu.VMEM((width, width), F32)],
        compiler_params=pltpu.CompilerParams(vmem_limit_bytes=VMEM_GRANT),
        cost_estimate=pl.CostEstimate(
            flops=60_000_000_000, bytes_accessed=16_000_000, transcendentals=0
        ),
        name="invert_gram",
    )(rows, after)


def merge_kernel(
    packed_hbm, maps_hbm, out_hbm, packed_ref, maps_ref, rows_ref, out_ref, sems, half_sems, out_sems
):
    groups = packed_ref.shape[0]
    size, width = out_ref.shape
    blocks = width // LANES
    kept = groups * KEPT * TILE
    arrivals = []
    for half in range(2):
        here = pl.ds(half * (groups // 2), groups // 2)
        arrivals.append(
            pltpu.make_async_copy(packed_hbm.at[here], packed_ref.at[here], half_sems.at[half])
        )
        arrivals[-1].start()
    copies = []
    for index in range(size // BLK):
        here = slice(2 * index * BLK, 2 * (index + 1) * BLK)
        copies.append(
            pltpu.make_async_copy(maps_hbm.at[here], maps_ref.at[here], sems.at[index])
        )
        copies[-1].start()
    count = groups // 2
    tall = kept // 2
    short = count * TILE // 2
    for half, arrival in enumerate(arrivals):
        arrival.wait()
        here = slice(half * count, (half + 1) * count)
        for block in range(blocks):
            lanes = slice(block * LANES, (block + 1) * LANES)
            rows = packed_ref[here, KEPT * block : KEPT * block + KEPT]
            rows_ref[half * tall : (half + 1) * tall, lanes] = rows.reshape(tall, LANES)
            last = packed_ref[here, KEPT * blocks + block % KEPT]
            last = last.reshape(count // 2, 2, TILE, LANES)
            at = kept + half * short
            rows_ref[at : at + short, lanes] = pair_ends(last[:, 0], last[:, 1], block >= KEPT)
    stores = []
    for index, copy in enumerate(copies):
        copy.wait()
        value = dot(maps_ref[2 * index * BLK : 2 * (index + 1) * BLK], rows_ref[...])
        here = slice(index * BLK, (index + 1) * BLK)
        out_ref[here] = (value[:BLK] + value[BLK:]).astype(BF16)
        stores.append(
            pltpu.make_async_copy(out_ref.at[here], out_hbm.at[here], out_sems.at[index])
        )
        stores[-1].start()
    for store in stores:
        store.wait()


def merge_rows(packed, maps):
    size, slots = maps.shape
    width = (packed.shape[1] // KEPT - 1) * LANES
    return pl.pallas_call(
        merge_kernel,
        out_shape=pltpu.HBM((size // 2, width), BF16),
        in_specs=[pl.BlockSpec(memory_space=pl.ANY)] * 2,
        out_specs=pl.BlockSpec(memory_space=pltpu.HBM),
        scratch_shapes=[
            pltpu.VMEM(packed.shape, BF16),
            pltpu.VMEM(maps.shape, BF16),
            pltpu.VMEM((slots, width), BF16),
            pltpu.VMEM((size // 2, width), BF16),
            pltpu.SemaphoreType.DMA((size // (2 * BLK),)),
            pltpu.SemaphoreType.DMA((2,)),
            pltpu.SemaphoreType.DMA((size // (2 * BLK),)),
        ],
        compiler_params=pltpu.CompilerParams(vmem_limit_bytes=VMEM_GRANT),
        cost_estimate=pl.CostEstimate(
            flops=9_400_000_000, bytes_accessed=16_000_000, transcendentals=0
        ),
        name="merge_rows",
    )(packed, maps)


def member_places(merge_group, group_count):
    experts = merge_group.shape[0]
    index = jnp.arange(experts, dtype=jnp.int32)
    earlier = index[None, :] < index[:, None]
    rank = jnp.sum(
        (merge_group[:, None] == merge_group[None, :]) & earlier, axis=1, dtype=jnp.int32
    )
    place = merge_group * GMAX + rank
    wanted = jnp.arange(group_count * GMAX, dtype=jnp.int32)
    members = jnp.sum(jnp.where(place[None, :] == wanted[:, None], index[None, :], 0), axis=1)
    chunk = merge_group * (OWNED * TILE)
    bases = [chunk + rank * TILE, chunk + GMAX * TILE + rank * (TILE // 2) - TILE]
    return members, jnp.stack(bases, axis=1)


def exchange(rows):
    return lax.all_to_all(rows, "expert", split_axis=0, concat_axis=0, tiled=True)


def on_device(routes, routed_hidden, down_proj, merge_group):
    group_count = lax.axis_size("expert")
    parts = lax.axis_size("mp")
    full_width, out_part = down_proj.shape[1:]
    tok_count, top_count, hidden_part = routed_hidden.shape
    row_count = tok_count * top_count
    experts = merge_group.shape[0]

    rows = routed_hidden.reshape(row_count, hidden_part)
    targets = routes.reshape(1, row_count)
    index = jnp.arange(experts, dtype=jnp.int32)
    chunk, local = index // 2 * (HELD * TILE), index % 2
    held_bases = jnp.stack(
        [chunk + local * TILE, chunk + 2 * TILE + local * (TILE // 2) - TILE], axis=1
    )
    members, owned_bases = member_places(merge_group, group_count)

    to_holder = pack_rows(
        targets, held_bases, rows, group_count * HELD * TILE, SMALL_GRANT, "pack_held"
    ).reshape(group_count, HELD * TILE, hidden_part)
    to_owner = pack_rows(
        targets, owned_bases, rows, group_count * OWNED * TILE, WIDE_GRANT, "pack_owned"
    ).reshape(group_count, OWNED * TILE, hidden_part)
    at_holder = exchange(to_holder)
    at_holder, to_owner = lax.optimization_barrier((at_holder, to_owner))
    held = lax.all_gather(at_holder, "mp", axis=0)
    at_owner = exchange(to_owner)

    projected = project_rows(
        held.reshape(parts, group_count, HELD, TILE, hidden_part), down_proj
    )
    home = exchange(projected.reshape(group_count, HELD * TILE, out_part))
    owned = lax.all_gather(at_owner, "mp", axis=0)
    regrouped = regroup_rows(home.reshape(group_count, HELD, TILE, out_part), members)
    arrived = exchange(regrouped)

    maps = invert_gram(
        owned.reshape(parts, group_count, OWNED, TILE, hidden_part), regrouped
    )
    merged = merge_rows(arrived, maps)
    return merged.reshape(1, full_width, out_part)


def solution(mesh):
    return jax.shard_map(
        on_device,
        mesh=mesh,
        in_specs=(P("expert", None), P("expert", None, "mp"), P("expert", None, "mp"), P()),
        out_specs=P("expert", None, "mp"),
        check_vma=False,
    )
```
